32 devices in a mesh: tm: 8 (over z, y), space: 4 (over x, core).
Axes of the slice: x: 2, y: 2, z: 4, core: 2. Of those that a mesh axis runs over, the one named last changes fastest.
Arguments:
- forcing: float32 [32, 128, 128, 128], P('tm', 'space'), may hold values from -6 to 6
- coarse_guess: float32 [8, 128, 128, 128], P('tm', 'space'), may hold values from -6 to 6
- initial: float32 [128, 128, 128], P('space'), may hold values from -6 to 6
Outputs:
- solution: float32 [32, 128, 128, 128], P('tm', 'space')
- residual: float32 [8, 128, 128, 128], P('tm', None, 'space')
The draws below stay inside these ranges and needn't reach their ends.
All inputs are finite; a program needn't handle non-finite values.
Results may differ from the reference program's by a relative error of at most 0.00007.
Values sent between devices are 32-bit elements; how exact they have to be, the bound alone decides.
No kernel may reach another device: no remote copies, remote signals or barrier semaphores. Data moves between devices by JAX's collectives and lax.ppermute only.
A program may use at most 192 MiB of HBM per device.

```python
import jax
import jax.numpy as jnp
from jax import lax

NX = 128
NY = 128
NZ = 128
COARSEN = 4
STEPS = 32
INTERVALS = 8
N_TM = 8


def levels(key, dims, shards, smallest, top_value):
    def one(position, shards_of):
        draws = jax.random.uniform(jax.random.fold_in(jax.random.fold_in(key, 6), position), (shards_of,), jnp.float32, smallest / len(shards), top_value / len(shards))
        return jnp.repeat(jnp.exp(draws), dims[position] // shards_of).reshape((-1,) + (1,) * (len(dims) - position - 1))

    factor_of = one(*shards[0])
    for cut in shards[1:]:
        factor_of = factor_of * one(*cut)
    return factor_of


def noise(key, extent, deviation, most, pieces=(), held_as=jnp.bfloat16):
    gain = levels(key, extent, pieces, -0.22, 0.18) if pieces else 1.0
    drawn = jax.random.normal(key, extent, jnp.float32) * deviation * gain
    return jnp.minimum(jnp.maximum(drawn, -most), most).astype(held_as)


def setup_inputs(seed: int = 0) -> dict:
    key_list = jax.random.split(jax.random.key(seed), 4)
    forcing = noise(key_list[0], (STEPS, NX, NY, NZ), 1.0, 6.0, ((0, 8), (1, 4)), jnp.float32)
    coarse_guess = noise(key_list[1], (INTERVALS, NX, NY, NZ), 1.0, 6.0, ((0, 8), (1, 4)), jnp.float32)
    initial = noise(key_list[2], (NX, NY, NZ), 1.0, 6.0, ((0, 4),), jnp.float32)
    return dict(forcing=forcing, coarse_guess=coarse_guess, initial=initial)


time_step = 0.5
highest = lax.Precision.HIGHEST

def sine_table(length):
    ladder = jnp.arange(1, length + 1, dtype=jnp.float32)
    return jnp.sqrt(2.0 / (length + 1)) * jnp.sin(jnp.pi * ladder[:, None] * ladder[None, :] / (length + 1))

def eigen_values(length):
    ladder = jnp.arange(1, length + 1, dtype=jnp.float32)
    return -4.0 * jnp.sin(jnp.pi * ladder / (2 * (length + 1))) ** 2

def all_modes(fields, table_x, table_y, table_z):
    fields = jnp.einsum('bxyz,zr->bxyr', fields, table_z, precision=highest)
    fields = jnp.einsum('bxyr,yq->bxqr', fields, table_y, precision=highest)
    return jnp.einsum('bxqr,xp->bpqr', fields, table_x, precision=highest)

def reference(forcing, coarse_guess, initial):
    table_x = sine_table(NX)
    table_y = sine_table(NY)
    table_z = sine_table(NZ)
    spectrum = eigen_values(NX)[:, None, None] + eigen_values(NY)[None, :, None] + eigen_values(NZ)[None, None, :]
    implicit = 1.0 - 0.5 * time_step * spectrum
    fine_rate = (1.0 + 0.5 * time_step * spectrum) / implicit
    wide_step = 0.5 * COARSEN * time_step
    coarse_rate = (1.0 + wide_step * spectrum) / (1.0 - wide_step * spectrum)
    blocks = forcing.reshape(N_TM, COARSEN, NX, NY, NZ)
    source = lax.map(lambda block: all_modes(block, table_x, table_y, table_z) * (time_step / implicit), blocks)
    anchor = all_modes(initial[None], table_x, table_y, table_z)
    firsts = jnp.concatenate([coarse_guess[-1:], coarse_guess[:-1]], axis=0)
    begin = lax.map(lambda field: all_modes(field[None], table_x, table_y, table_z)[0], firsts)

    def relax_steps(starting):
        current = starting
        values = []
        for number in range(COARSEN - 1):
            current = fine_rate * current + source[:, number]
            values.append(current)
        return values
    coarse_value = fine_rate * relax_steps(begin)[-1] + source[:, COARSEN - 1]
    second = jnp.concatenate([anchor, coarse_value[:-1]], axis=0)
    residual = fine_rate * relax_steps(second)[-1] + source[:, COARSEN - 1] - coarse_value

    def sweep(error, term):
        error = coarse_rate * error + term
        return (error, error)
    _, errors = lax.scan(sweep, jnp.zeros_like(anchor[0]), residual)
    corrected = coarse_value + errors
    third = jnp.concatenate([anchor, corrected[:-1]], axis=0)
    points = relax_steps(third) + [corrected]
    stacked = jnp.stack(points, axis=1)
    cells = lax.map(lambda block: all_modes(block, table_x, table_y, table_z), stacked)
    return (cells.reshape(COARSEN * N_TM, NX, NY, NZ), residual)
```

```python
import functools

import jax
import jax.numpy as jnp
import numpy as np
from jax import lax
from jax.experimental import pallas as pl
from jax.experimental.pallas import tpu as pltpu
from jax.sharding import Mesh
from jax.sharding import PartitionSpec as P

time_step = 0.5
half = 0.5 * time_step
high = lax.Precision.HIGH


def sine_table(length):
    ladder = np.arange(1, length + 1, dtype=np.float64)
    table = np.sqrt(2.0 / (length + 1)) * np.sin(
        np.pi * ladder[:, None] * ladder[None, :] / (length + 1)
    )
    return table.astype(np.float32)


def eigen_values(length):
    ladder = np.arange(1, length + 1, dtype=np.float64)
    return -4.0 * np.sin(np.pi * ladder / (2 * (length + 1))) ** 2


def pivot_table(planes, width_y, width_z):
    cross = eigen_values(width_y)[:, None] + eigen_values(width_z)[None, :]
    diagonal = 1.0 + 2.0 * half - half * cross
    pivots = [1.0 / diagonal]
    for _ in range(planes - 1):
        pivots.append(1.0 / (diagonal - half * half * pivots[-1]))
    return np.stack(pivots).astype(np.float32)


def eliminate(planes, right, pivots, ghosts=None):
    forward = []
    for k in range(planes):
        value = right(k)
        if k > 0:
            value = value + half * forward[-1]
        elif ghosts is not None:
            value = value + half * ghosts[0]
        if k == planes - 1 and ghosts is not None:
            value = value + half * ghosts[1]
        forward.append(value * pivots[k])
    solved = [None] * planes
    solved[-1] = forward[-1]
    for k in range(planes - 2, -1, -1):
        solved[k] = forward[k] + (half * pivots[k]) * solved[k + 1]
    return solved


def relax_kernel(forcing_ref, pivot_ref, out_ref, work):
    steps, planes = forcing_ref.shape[:2]
    for n in range(steps):

        def right(k):
            pushed = time_step * forcing_ref[n, k]
            return pushed if n == 0 else pushed + 2.0 * out_ref[k]

        forward = None
        for k in range(planes):
            value = right(k)
            if k > 0:
                value = value + half * forward
            forward = value * pivot_ref[k]
            work[k] = forward
        solved = None
        for k in range(planes - 1, -1, -1):
            if k == planes - 1:
                solved = work[k]
            else:
                solved = work[k] + (half * pivot_ref[k]) * solved
            if k == planes - 1:
                out_ref[planes + 2 * n + 1] = solved
            if k == 0:
                out_ref[planes + 2 * n] = solved
            out_ref[k] = solved if n == 0 else solved - out_ref[k]


def finish_kernel(forcing_ref, start_ref, ghost_ref, pivot_ref, out_ref, work):
    steps, planes = out_ref.shape[:2]
    for n in range(steps):
        old = (lambda k: start_ref[k]) if n == 0 else (lambda k: out_ref[n - 1, k])
        forward = None
        for k in range(planes):
            value = time_step * forcing_ref[n, k] + 2.0 * old(k)
            if k > 0:
                value = value + half * forward
            else:
                value = value + half * ghost_ref[2 * n]
            if k == planes - 1:
                value = value + half * ghost_ref[2 * n + 1]
            forward = value * pivot_ref[k]
            work[k] = forward
        solved = None
        for k in range(planes - 1, -1, -1):
            if k == planes - 1:
                solved = work[k]
            else:
                solved = work[k] + (half * pivot_ref[k]) * solved
            out_ref[n, k] = solved - old(k)


def rows_block(width):
    return next(rows for rows in (32, 16, 8, width) if width % rows == 0)


def local_relax(forcing, pivots):
    steps, planes, width_y, width_z = forcing.shape
    rows = rows_block(width_y)
    return pl.pallas_call(
        relax_kernel,
        grid=(width_y // rows,),
        out_shape=jax.ShapeDtypeStruct((planes + 2 * steps, width_y, width_z), jnp.float32),
        in_specs=[
            pl.BlockSpec((steps, planes, rows, width_z), lambda i: (0, 0, i, 0)),
            pl.BlockSpec((planes, rows, width_z), lambda i: (0, i, 0)),
        ],
        out_specs=pl.BlockSpec((planes + 2 * steps, rows, width_z), lambda i: (0, i, 0)),
        scratch_shapes=[pltpu.VMEM((planes, rows, width_z), jnp.float32)],
        compiler_params=pltpu.CompilerParams(vmem_limit_bytes=48 << 20),
    )(forcing, pivots)


def local_finish(forcing, start, ghosts, pivots):
    steps, planes, width_y, width_z = forcing.shape
    rows = rows_block(width_y)
    return pl.pallas_call(
        finish_kernel,
        grid=(width_y // rows,),
        out_shape=jax.ShapeDtypeStruct((steps - 1, planes, width_y, width_z), jnp.float32),
        in_specs=[
            pl.BlockSpec((steps, planes, rows, width_z), lambda i: (0, 0, i, 0)),
            pl.BlockSpec((planes, rows, width_z), lambda i: (0, i, 0)),
            pl.BlockSpec((2 * (steps - 1), rows, width_z), lambda i: (0, i, 0)),
            pl.BlockSpec((planes, rows, width_z), lambda i: (0, i, 0)),
        ],
        out_specs=pl.BlockSpec((steps - 1, planes, rows, width_z), lambda i: (0, 0, i, 0)),
        scratch_shapes=[pltpu.VMEM((planes, rows, width_z), jnp.float32)],
        compiler_params=pltpu.CompilerParams(vmem_limit_bytes=48 << 20),
    )(forcing, start, ghosts, pivots)


def per_device(forcing, coarse_guess, initial):
    steps, planes, width_y, width_z = forcing.shape
    n_space = lax.axis_size("space")
    n_plane = lax.axis_size("plane")
    width_x = planes * n_space
    parts = 2 * n_space
    own = width_y // parts
    table_x, table_y, table_z = (jnp.asarray(sine_table(n)) for n in (width_x, width_y, width_z))
    pivots = jnp.asarray(pivot_table(planes, width_y, width_z))
    pair = lax.axis_index("pair")
    level = lax.axis_index("plane")
    offset = (lax.axis_index("space") * 2 + pair) * own
    e_x, e_y, e_z = (
        jnp.asarray(eigen_values(n).astype(np.float32)) for n in (width_x, width_y, width_z)
    )
    spectrum = (
        e_x[:, None, None]
        + lax.dynamic_slice_in_dim(e_y, offset, own)[None, :, None]
        + e_z[None, None, :]
    )
    implicit = 1.0 - half * spectrum
    fine = (1.0 + half * spectrum) / implicit
    wide = steps * half
    coarse = (1.0 + wide * spectrum) / (1.0 - wide * spectrum)
    power = [jnp.ones_like(fine)]
    for _ in range(steps):
        power.append(power[-1] * fine)
    leap = power[steps]

    def inward(fields, table_q):
        fields = jnp.einsum("bxyz,zr->bxyr", fields, table_z, precision=high)
        return jnp.einsum("bxyr,yq->bxqr", fields, table_q, precision=high)

    def spread(fields):
        cut = fields.reshape(fields.shape[0], parts, own, width_z)
        got = lax.all_to_all(cut, ("space", "pair"), split_axis=1, concat_axis=0)
        return got.reshape(n_space, 2, fields.shape[0], own, width_z)

    def collect(fields):
        count = fields.shape[2]
        cut = fields.reshape(parts, count, own, width_z)
        got = lax.all_to_all(cut, ("space", "pair"), split_axis=0, concat_axis=1)
        return got.reshape(count, width_y, width_z)

    def modes(cells):
        return jnp.einsum(
            "sbmqr,smp->bpqr", cells, table_x.reshape(n_space, planes, width_x), precision=high
        )

    guess = modes(spread(inward(coarse_guess, table_y)[0]))
    before = lax.ppermute(guess[1], "plane", [(i, (i + 1) % n_plane) for i in range(n_plane)])

    lines = table_y.reshape(width_y, n_space, 2, own)
    lines = lax.dynamic_index_in_dim(lines, pair, 2, False).reshape(width_y, n_space * own)
    opening = inward(initial[None], lines)[0].reshape(planes, n_space, own, width_z)
    opening = lax.all_to_all(opening, "space", split_axis=1, concat_axis=0)
    anchor = jnp.einsum(
        "smqr,smp->pqr", opening, table_x.reshape(n_space, planes, width_x), precision=high
    )

    pushed = inward(forcing, table_y)
    arrived = spread(local_relax(pushed, pivots))
    edges = arrived[:, :, planes:].reshape(n_space, 2, steps, 2, own, width_z)
    full = np.concatenate([np.zeros((1, width_x)), sine_table(width_x), np.zeros((1, width_x))])
    across = np.stack([full[0 : width_x : planes], full[planes + 1 :: planes]], axis=1)
    border = np.stack([full[1 : width_x + 1 : planes], full[planes : width_x + 1 : planes]], axis=1)
    across = jnp.asarray(across.astype(np.float32))
    border = jnp.asarray(border.astype(np.float32))
    kicks = jnp.einsum("sbnkqr,skp->nbpqr", edges, across, precision=high) * (half / implicit)
    drift = [kicks[0]]
    for n in range(1, steps):
        drift.append(fine * drift[-1] + kicks[n])
    gathered = modes(arrived[:, :, :planes]) + drift[-1]

    value = jnp.stack([leap * before + gathered[0], leap * guess[0] + gathered[1]])
    last = lax.ppermute(value[1], "plane", [(i, i + 1) for i in range(n_plane - 1)])
    last = jnp.where(level == 0, anchor, last)
    first_residual = leap * (last - before)
    second_residual = leap * (value[0] - guess[0])

    mine = jnp.where(pair == 0, first_residual, second_residual)
    other = jnp.where(pair == 0, second_residual, first_residual)
    other = lax.ppermute(other, "pair", [(0, 1), (1, 0)])
    residual = jnp.concatenate(
        [jnp.where(pair == 0, mine, other), jnp.where(pair == 0, other, mine)], axis=1
    )

    carried = jnp.zeros_like(last)
    for hop in range(n_plane - 1):
        sent = coarse * (coarse * carried + first_residual) + second_residual
        carried = carried + lax.ppermute(sent, "plane", [(hop, hop + 1)])
    error = coarse * carried + first_residual
    begin = jnp.stack([last + carried, value[0] + error])
    ends = jnp.stack([value[0] + error, value[1] + coarse * error + second_residual])

    bounds = []
    for n in range(1, steps):
        both = drift[n - 1] + (power[n] + power[n - 1]) * begin
        if n > 1:
            both = both + drift[n - 2]
        planes_of = jnp.einsum("bpqr,skp->sbkqr", both, border, precision=high) + edges[:, :, n - 1]
        blank = jnp.zeros_like(planes_of[:1, :, 0])
        left = jnp.concatenate([blank, planes_of[:-1, :, 1]], axis=0)
        right = jnp.concatenate([planes_of[1:, :, 0], blank], axis=0)
        bounds += [left[:, :, None], right[:, :, None]]

    def cells(spectra):
        return jnp.einsum(
            "bpqr,smp->sbmqr", spectra, table_x.reshape(n_space, planes, width_x), precision=high
        )

    returned = collect(jnp.concatenate([cells(begin), cells(ends)] + bounds, axis=2))
    points = local_finish(pushed, returned[:planes], returned[2 * planes :], pivots)
    points = jnp.concatenate([points, returned[None, planes : 2 * planes]], axis=0)
    points = jnp.einsum("bxqr,qy->bxyr", points, table_y, precision=high)
    return (jnp.einsum("bxyr,rz->bxyz", points, table_z, precision=high), residual[None])


def solution(mesh):
    whole = mesh.devices
    split = Mesh(whole.reshape(whole.shape[0] // 2, 2, whole.shape[1]), ("plane", "pair", "space"))
    both = ("plane", "pair")
    placed = (P(both, "space", None, None), P(both, "space", None, None), P("space", None, None))
    return jax.shard_map(
        per_device,
        mesh=split,
        in_specs=placed,
        out_specs=(P(both, "space", None, None), P(both, None, "space", None)),
        check_vma=False,
    )
```

```python
import jax
import jax.numpy as jnp
import ml_dtypes
import numpy as np
from jax import lax
from jax.experimental import pallas as pl
from jax.experimental.pallas import tpu as pltpu
from jax.sharding import Mesh
from jax.sharding import PartitionSpec as P

time_step = 0.5
half = 0.5 * time_step
high = lax.Precision.HIGH


def room(mebibytes):
    return pltpu.CompilerParams(vmem_limit_bytes=mebibytes << 20)


def cost(*arrays):
    moved = sum(int(np.prod(a.shape)) * 4 for a in arrays)
    return pl.CostEstimate(flops=moved * 400, bytes_accessed=2 * moved, transcendentals=0)


def sine_table(length):
    ladder = np.arange(1, length + 1, dtype=np.float64)
    table = np.sqrt(2.0 / (length + 1)) * np.sin(
        np.pi * ladder[:, None] * ladder[None, :] / (length + 1)
    )
    return table.astype(np.float32)


def eigen_values(length):
    ladder = np.arange(1, length + 1, dtype=np.float64)
    return -4.0 * np.sin(np.pi * ladder / (2 * (length + 1))) ** 2


def two_parts(table):
    upper = table.astype(ml_dtypes.bfloat16)
    return upper, (table - upper.astype(np.float32)).astype(ml_dtypes.bfloat16)


def right_table(table):
    upper, lower = two_parts(table)
    return np.block([[upper, lower], [upper, np.zeros_like(lower)]])


def left_table(table):
    upper, lower = two_parts(table)
    return np.block([[upper, upper], [lower, np.zeros_like(lower)]])


def pivot_table(planes, width_y, width_z, weight):
    cross = eigen_values(width_y)[:, None] + eigen_values(width_z)[None, :]
    diagonal = (1.0 + 2.0 * weight - weight * cross) / weight
    pivots = [1.0 / diagonal]
    for _ in range(planes // 2 - 1):
        pivots.append(1.0 / (diagonal - pivots[-1]))
    pivots.append(1.0 / (1.0 - pivots[-1] ** 2))
    return np.stack(pivots).astype(np.float32)


def split(values):
    upper = values.astype(jnp.bfloat16)
    return upper, (values - upper.astype(jnp.float32)).astype(jnp.bfloat16)


def times_right(values, table):
    width = values.shape[-1]
    both = jnp.dot(
        jnp.concatenate(split(values), axis=1), table, preferred_element_type=jnp.float32
    )
    return both[:, :width] + both[:, width:]


def times_left(table, values):
    both = jnp.dot(
        table, jnp.concatenate(split(values), axis=0), preferred_element_type=jnp.float32
    )
    width = values.shape[0]
    return both[:width] + both[width:]


def solve(planes, right, pivot, work, left_ghost, right_ghost, finish):
    middle = planes // 2
    lower, upper = left_ghost, right_ghost
    for k in range(middle):
        low, top = right(k), right(planes - 1 - k)
        low = low if lower is None else low + lower
        top = top if upper is None else top + upper
        factor = pivot(k)
        lower, upper = low * factor, top * factor
        if k < middle - 1:
            work[k] = lower
            work[planes - 1 - k] = upper
    factor, joint = pivot(middle - 1), pivot(middle)
    lower, upper = (lower + factor * upper) * joint, (upper + factor * lower) * joint
    finish(middle - 1, lower)
    finish(planes - middle, upper)
    for k in range(middle - 2, -1, -1):
        factor = pivot(k)
        lower = work[k] + factor * lower
        upper = work[planes - 1 - k] + factor * upper
        finish(k, lower)
        finish(planes - 1 - k, upper)


def transformed(block, z_ref, y_ref):
    count, width_y, width_z = block.shape
    lines = times_right(block.reshape(count * width_y, width_z), z_ref[...])
    step = 2 if count % 2 == 0 else 1
    out = []
    for i in range(0, count, step):
        wide = [lines[(i + j) * width_y : (i + j + 1) * width_y] for j in range(step)]
        wide = times_left(y_ref[...], jnp.concatenate(wide, axis=1))
        out += [wide[:, j * width_z : (j + 1) * width_z] for j in range(step)]
    return out


def front_kernel(x_steps, forcing_ref, z_ref, y_ref, pivot_ref, pushed_ref, out_ref, kept, work):
    steps, count, width_y, width_z = forcing_ref.shape
    planes, parts, own = kept.shape[1:4]
    some = out_ref.shape[0]
    turn = pl.program_id(0)

    @pl.when(turn < x_steps)
    def _():
        for n in range(steps):
            for i, plane in enumerate(transformed(forcing_ref[n], z_ref, y_ref)):
                pushed_ref[n, i] = plane
                kept[n, turn * count + i] = plane.reshape(parts, own, width_z)

    @pl.when(turn >= x_steps)
    def _():
        place = pl.ds((turn - x_steps) * some, some)
        for n in range(steps):

            def right(k):
                pushed = kept[n, k, place]
                return pushed if n == 0 else pushed + (2.0 / half) * out_ref[:, k]

            def finish(k, solved):
                if k == 0:
                    out_ref[:, planes + 2 * n] = solved
                if k == planes - 1:
                    out_ref[:, planes + 2 * n + 1] = solved
                out_ref[:, k] = solved if n == 0 else solved - out_ref[:, k]

            solve(planes, right, lambda k: pivot_ref[k], work, None, None, finish)


def front(forcing, z_right, y_left, pivots, parts):
    steps, planes, width_y, width_z = forcing.shape
    own = width_y // parts
    count = 4 if planes % 4 == 0 else 1
    some = 2 if parts % 2 == 0 else 1
    x_steps, q_steps = planes // count, parts // some
    early = lambda i: jnp.minimum(i, x_steps - 1)
    late = lambda i: jnp.maximum(i - x_steps, 0)
    total = planes + 2 * steps
    return pl.pallas_call(
        lambda *refs: front_kernel(x_steps, *refs),
        grid=(x_steps + q_steps,),
        out_shape=(
            jax.ShapeDtypeStruct(forcing.shape, jnp.float32),
            jax.ShapeDtypeStruct((parts, total, own, width_z), jnp.float32),
        ),
        in_specs=[
            pl.BlockSpec((steps, count, width_y, width_z), lambda i: (0, early(i), 0, 0)),
            pl.BlockSpec(z_right.shape, lambda i: (0, 0)),
            pl.BlockSpec(y_left.shape, lambda i: (0, 0)),
            pl.BlockSpec((planes // 2 + 1, some, own, width_z), lambda i: (0, late(i), 0, 0)),
        ],
        out_specs=(
            pl.BlockSpec((steps, count, width_y, width_z), lambda i: (0, early(i), 0, 0)),
            pl.BlockSpec((some, total, own, width_z), lambda i: (late(i), 0, 0, 0)),
        ),
        scratch_shapes=[
            pltpu.VMEM((steps, planes, parts, own, width_z), jnp.float32),
            pltpu.VMEM((planes, some, own, width_z), jnp.float32),
        ],
        cost_estimate=cost(forcing),
        compiler_params=room(24),
    )(forcing, z_right, y_left, pivots)


def opening_kernel(g_steps, pair_ref, guess_ref, initial_ref, z_ref, y_ref, out_ref):
    parts, count, own, width_z = out_ref.shape
    block = jnp.where(pl.program_id(0) < g_steps, guess_ref[...], initial_ref[...])
    for i, plane in enumerate(transformed(block, z_ref, y_ref)):
        out_ref[:, i] = plane.reshape(parts, own, width_z)


def opening_fields(guess, initial, z_right, y_left, pair, parts):
    planes, width_y, width_z = guess.shape
    share = planes // 2
    count = 8 if share % 8 == 0 else 1
    g_steps, a_steps = planes // count, share // count
    own = width_y // parts
    block = (count, width_y, width_z)
    whole = lambda a: pl.BlockSpec(a.shape, lambda i, p: (0, 0))
    return pl.pallas_call(
        lambda *refs: opening_kernel(g_steps, *refs),
        grid_spec=pltpu.PrefetchScalarGridSpec(
            num_scalar_prefetch=1,
            grid=(g_steps + a_steps,),
            in_specs=[
                pl.BlockSpec(block, lambda i, p: (jnp.minimum(i, g_steps - 1), 0, 0)),
                pl.BlockSpec(
                    block, lambda i, p: (p[0] * a_steps + jnp.maximum(i - g_steps, 0), 0, 0)
                ),
                whole(z_right),
                whole(y_left),
            ],
            out_specs=pl.BlockSpec((parts, count, own, width_z), lambda i, p: (0, i, 0, 0)),
        ),
        out_shape=jax.ShapeDtypeStruct((parts, planes + share, own, width_z), jnp.float32),
        cost_estimate=cost(guess),
        compiler_params=room(60),
    )(pair[None], guess, initial, z_right, y_left)


def relax_kernel(pushed_ref, early_ref, fine_ref, out_ref, work):
    steps, planes = out_ref.shape[:2]
    for n in range(steps):

        def old(k):
            return early_ref[:, k] if n == 0 else out_ref[n - 1, k]

        def right(k):
            return pushed_ref[n, k] + (2.0 / half) * old(k)

        def keep(k, solved):
            out_ref[n, k] = solved - old(k)

        ghosts = [early_ref[:, planes + 2 * n + i] for i in (0, 1)]
        solve(planes, right, lambda k: fine_ref[k], work, *ghosts, keep)


def relax(pushed, early, fine_pivots):
    steps, planes, parts, own, width_z = pushed.shape
    step = 2 if parts % 2 == 0 else 1
    block = pl.BlockSpec((steps, planes, step, own, width_z), lambda i: (0, 0, i, 0, 0))
    return pl.pallas_call(
        relax_kernel,
        grid=(parts // step,),
        out_shape=jax.ShapeDtypeStruct(pushed.shape, jnp.float32),
        in_specs=[
            block,
            pl.BlockSpec((step, early.shape[1], own, width_z), lambda i: (i, 0, 0, 0)),
            pl.BlockSpec((planes // 2 + 1, step, own, width_z), lambda i: (0, i, 0, 0)),
        ],
        out_specs=block,
        scratch_shapes=[pltpu.VMEM((planes, step, own, width_z), jnp.float32)],
        cost_estimate=cost(early),
        compiler_params=room(24),
    )(pushed, early, fine_pivots)


def finish_kernel(q_steps, relaxed_ref, *refs):
    *late_refs, fine_ref, wide_ref, y_ref, z_ref, out_ref, points, state, work = refs
    steps, count, width_y, width_z = out_ref.shape
    planes = points.shape[1]
    some = state.shape[1]
    wide = steps * half
    turn = pl.program_id(0)

    def late(k):
        return jnp.concatenate([ref[:, k] for ref in late_refs], axis=1)

    @pl.when(turn < q_steps)
    def _():
        place = pl.ds(turn * some, some)

        def sent(k, solved):
            points[steps - 1, k, place] = relaxed_ref[steps - 1, k] + (solved - late(k))

        ghosts = [late(planes + 2 * (steps - 1) + i) for i in (0, 1)]
        solve(planes, lambda k: (2.0 / wide) * late(k), lambda k: wide_ref[k], work, *ghosts, sent)
        for n in range(steps - 1):

            def old(k):
                return late(k) if n == 0 else state[k]

            def right(k):
                return (2.0 / half) * old(k)

            def keep(k, solved):
                fresh = solved - old(k)
                state[k] = fresh
                points[n, k, place] = relaxed_ref[n, k] + fresh

            ghosts = [late(planes + 2 * n + i) for i in (0, 1)]
            solve(planes, right, lambda k: fine_ref[k], work, *ghosts, keep)

    @pl.when(turn >= q_steps)
    def _():
        first = (turn - q_steps) * count
        step = 2 if count % 2 == 0 else 1
        for n in range(steps):
            lines = []
            for i in range(0, count, step):
                wide = [points[n, first + i + j].reshape(width_y, width_z) for j in range(step)]
                wide = times_left(y_ref[...], jnp.concatenate(wide, axis=1))
                lines += [wide[:, j * width_z : (j + 1) * width_z] for j in range(step)]
            block = times_right(jnp.concatenate(lines, axis=0), z_ref[...])
            out_ref[n] = block.reshape(count, width_y, width_z)


def finish(relaxed, lates, fine_pivots, wide_pivots, y_left, z_right):
    steps, planes, parts, own, width_z = relaxed.shape
    width_y = parts * own
    some = 2 if parts % 2 == 0 else 1
    count = 4 if planes % 4 == 0 else 1
    q_steps, x_steps = parts // some, planes // count
    ahead = lambda i: jnp.minimum(i, q_steps - 1)
    after = lambda i: jnp.maximum(i - q_steps, 0)
    pivots = pl.BlockSpec((planes // 2 + 1, some, own, width_z), lambda i: (0, ahead(i), 0, 0))
    return pl.pallas_call(
        lambda *refs: finish_kernel(q_steps, *refs),
        grid=(q_steps + x_steps,),
        out_shape=jax.ShapeDtypeStruct((steps, planes, width_y, width_z), jnp.float32),
        in_specs=[
            pl.BlockSpec((steps, planes, some, own, width_z), lambda i: (0, 0, ahead(i), 0, 0)),
            *(
                pl.BlockSpec((some, *late.shape[1:]), lambda i: (ahead(i), 0, 0, 0))
                for late in lates
            ),
            pivots,
            pivots,
            pl.BlockSpec(y_left.shape, lambda i: (0, 0)),
            pl.BlockSpec(z_right.shape, lambda i: (0, 0)),
        ],
        out_specs=pl.BlockSpec((steps, count, width_y, width_z), lambda i: (0, after(i), 0, 0)),
        scratch_shapes=[
            pltpu.VMEM(relaxed.shape, jnp.float32),
            pltpu.VMEM((planes, some, own, width_z), jnp.float32),
            pltpu.VMEM((planes, some, own, width_z), jnp.float32),
        ],
        cost_estimate=cost(relaxed),
        compiler_params=room(28),
    )(relaxed, *lates, fine_pivots, wide_pivots, y_left, z_right)


def per_device(forcing, coarse_guess, initial):
    steps, planes, width_y, width_z = forcing.shape
    n_space = lax.axis_size("space")
    n_plane = lax.axis_size("plane")
    width_x = planes * n_space
    parts = 2 * n_space
    own = width_y // parts
    chunks = 2 if own % 16 == 0 else 1
    rows = own // chunks
    table_x = jnp.asarray(sine_table(width_x))
    z_right = jnp.asarray(right_table(sine_table(width_z)))
    y_left = jnp.asarray(left_table(sine_table(width_y)))
    y_scaled = jnp.asarray(left_table((time_step / half) * sine_table(width_y)))
    fine_pivots = pivot_table(planes, width_y, width_z, half)
    wide_pivots = pivot_table(planes, width_y, width_z, steps * half)
    pair = lax.axis_index("pair")
    level = lax.axis_index("plane")
    offset = (lax.axis_index("space") * 2 + pair) * own
    e_x, e_y, e_z = (
        jnp.asarray(eigen_values(n).astype(np.float32)) for n in (width_x, width_y, width_z)
    )
    spectrum = (
        e_x[:, None, None]
        + lax.dynamic_slice_in_dim(e_y, offset, own)[None, :, None]
        + e_z[None, None, :]
    )
    implicit = 1.0 - half * spectrum
    fine = (1.0 + half * spectrum) / implicit
    wide = steps * half
    coarse = (1.0 + wide * spectrum) / (1.0 - wide * spectrum)
    power = [jnp.ones_like(fine)]
    for _ in range(steps):
        power.append(power[-1] * fine)
    leap = power[steps]

    def swap(fields):
        return lax.all_to_all(fields, ("space", "pair"), split_axis=0, concat_axis=0, tiled=True)

    def spread(fields):
        return swap(fields).reshape(n_space, 2, *fields.shape[1:])

    by_device = table_x.reshape(n_space, planes, width_x)

    def modes(cells):
        return jnp.einsum("sbmqr,smp->bpqr", cells, by_device, precision=high)

    share = planes // 2
    opened = opening_fields(coarse_guess[0], initial, z_right, y_left, pair, parts)
    opened, forcing = lax.optimization_barrier((opened, forcing))
    opened = spread(opened)
    pushed, relaxed = front(
        forcing, z_right, y_scaled, jnp.asarray(fine_pivots.reshape(-1, parts, own, width_z)), parts
    )
    opened, relaxed = lax.optimization_barrier((opened, relaxed))
    arrived = spread(relaxed)

    guess = modes(opened[:, :, :planes])
    before = lax.ppermute(guess[1], "plane", [(i, (i + 1) % n_plane) for i in range(n_plane)])
    anchor = jnp.einsum(
        "sbmqr,sbmp->pqr",
        opened[:, :, planes:],
        table_x.reshape(n_space, 2, share, width_x),
        precision=high,
    )

    edges = arrived[:, :, planes:].reshape(n_space, 2, steps, 2, own, width_z)
    full = np.concatenate([np.zeros((1, width_x)), sine_table(width_x), np.zeros((1, width_x))])
    across = np.stack([full[0 : width_x : planes], full[planes + 1 :: planes]], axis=1)
    border = np.stack([full[1 : width_x + 1 : planes], full[planes : width_x + 1 : planes]], axis=1)
    across = jnp.asarray(across.astype(np.float32))
    border = jnp.asarray(border.astype(np.float32))
    kicks = jnp.einsum("sbnkqr,skp->nbpqr", edges, across, precision=high) * (half / implicit)
    drift = [kicks[0]]
    for n in range(1, steps):
        drift.append(fine * drift[-1] + kicks[n])
    gathered = modes(arrived[:, :, :planes]) + drift[-1]

    value = jnp.stack([leap * before + gathered[0], leap * guess[0] + gathered[1]])
    second_residual = leap * (value[0] - guess[0])

    def chunk_of(array, c):
        return lax.slice_in_dim(array, c * rows, (c + 1) * rows, axis=array.ndim - 2)

    shifted = [
        lax.ppermute(chunk_of(value[1], c), "plane", [(i, i + 1) for i in range(n_plane - 1)])
        for c in range(chunks)
    ]
    rate = [chunk_of(coarse, c) for c in range(chunks)]
    second = [chunk_of(second_residual, c) for c in range(chunks)]
    start = [chunk_of(before, c) for c in range(chunks)]
    carries = [jnp.zeros_like(start[0])] * chunks
    lasts, firsts, sent = [], [], []

    def onward(c, carried):
        return rate[c] * (rate[c] * carried + firsts[c]) + second[c]

    def hop(c, sent, place):
        return lax.ppermute(sent, "plane", [(place, place + 1)])

    for c in range(chunks):
        if c > 0:
            sent[c - 1], start[c] = lax.optimization_barrier((sent[c - 1], start[c]))
        lasts.append(jnp.where(level == 0, chunk_of(anchor, c), shifted[c]))
        firsts.append(chunk_of(leap, c) * (lasts[c] - start[c]))
        sent.append(onward(c, carries[c]))
    sent[-1], lasts, firsts = lax.optimization_barrier((sent[-1], lasts, firsts))
    last = jnp.concatenate(lasts, axis=1)
    first_residual = jnp.concatenate(firsts, axis=1)

    def cells(spectra):
        return jnp.einsum("bpqr,smp->sbmqr", spectra, by_device, precision=high)

    def ghosts(spectra, own_planes=None):
        rim = jnp.einsum("nbpqr,skp->sbnkqr", spectra, border, precision=high)
        if own_planes is not None:
            rim = rim + own_planes
        blank = jnp.zeros_like(rim[:1, :, :, :1])
        left = jnp.concatenate([blank, rim[:-1, :, :, 1:]], axis=0)
        right = jnp.concatenate([rim[1:, :, :, :1], blank], axis=0)
        both = jnp.concatenate([left, right], axis=3)
        return both.reshape(n_space, 2, -1, *both.shape[4:])

    def sums(begin, count, c=None):
        pick = (lambda a: a) if c is None else (lambda a: chunk_of(a, c))
        return [pick(power[n] + power[n - 1]) * begin for n in range(1, count + 1)]

    def packed(*pieces):
        joined = jnp.concatenate(pieces, axis=2)
        return joined.reshape(parts, *joined.shape[2:])

    begin = jnp.stack([last, value[0]])
    both = sums(begin, steps)
    for n in range(steps):
        both[n] = both[n] + drift[n] + (drift[n - 1] if n > 0 else 0.0)
    early = packed(cells(begin), ghosts(jnp.stack(both), edges))
    mine = jnp.where(pair == 0, first_residual, second_residual)
    other = jnp.where(pair == 0, second_residual, first_residual)
    early, second, other = lax.optimization_barrier((early, second, other))
    other = lax.ppermute(other, "pair", [(0, 1), (1, 0)])
    early = swap(early)
    for place in range(n_plane - 1):
        for c in range(chunks):
            if place > 0:
                sent[c] = onward(c, carries[c])
        if place == n_plane - 2:
            sent, pushed = lax.optimization_barrier((sent, pushed))
        for c in range(chunks):
            carries[c] = carries[c] + hop(c, sent[c], place)
    fine_pivots, wide_pivots = (
        jnp.asarray(a.reshape(-1, parts, own, width_z)) for a in (fine_pivots, wide_pivots)
    )
    relaxed = relax(pushed.reshape(steps, planes, parts, own, width_z), early, fine_pivots)
    lates = []
    for c in range(chunks):
        error = jnp.stack([carries[c], rate[c] * carries[c] + firsts[c]])
        spectra = jnp.stack(sums(error, steps - 1, c) + [(rate[c] + 1.0) * error])
        late = packed(cells(error), ghosts(spectra))
        late, relaxed, mine = lax.optimization_barrier((late, relaxed, mine))
        lates.append(swap(late))
    residual = jnp.concatenate(
        [jnp.where(pair == 0, mine, other), jnp.where(pair == 0, other, mine)], axis=1
    )
    points = finish(relaxed, lates, fine_pivots, wide_pivots, y_left, z_right)
    return (points, residual[None])


def solution(mesh):
    whole = mesh.devices
    cut = Mesh(whole.reshape(whole.shape[0] // 2, 2, whole.shape[1]), ("plane", "pair", "space"))
    both = ("plane", "pair")
    placed = (P(both, "space", None, None), P(both, "space", None, None), P("space", None, None))
    return jax.shard_map(
        per_device,
        mesh=cut,
        in_specs=placed,
        out_specs=(P(both, "space", None, None), P(both, None, "space", None)),
        check_vma=False,
    )
```

```python
import jax
import jax.numpy as jnp
import ml_dtypes
import numpy as np
from jax import lax
from jax.experimental import pallas as pl
from jax.experimental.pallas import tpu as pltpu
from jax.sharding import Mesh
from jax.sharding import PartitionSpec as P

time_step = 0.5
half = 0.5 * time_step
high = lax.Precision.HIGH


def room(mebibytes):
    return pltpu.CompilerParams(vmem_limit_bytes=mebibytes << 20)


def cost(*arrays):
    moved = sum(int(np.prod(a.shape)) * 4 for a in arrays)
    return pl.CostEstimate(flops=moved * 400, bytes_accessed=2 * moved, transcendentals=0)


def sine_table(length):
    ladder = np.arange(1, length + 1, dtype=np.float64)
    table = np.sqrt(2.0 / (length + 1)) * np.sin(
        np.pi * ladder[:, None] * ladder[None, :] / (length + 1)
    )
    return table.astype(np.float32)


def eigen_values(length):
    ladder = np.arange(1, length + 1, dtype=np.float64)
    return -4.0 * np.sin(np.pi * ladder / (2 * (length + 1))) ** 2


def two_parts(table):
    upper = table.astype(ml_dtypes.bfloat16)
    return upper, (table - upper.astype(np.float32)).astype(ml_dtypes.bfloat16)


def right_table(table):
    upper, lower = two_parts(table)
    return np.block([[upper, lower], [upper, np.zeros_like(lower)]])


def left_table(table):
    upper, lower = two_parts(table)
    return np.block([[upper, upper], [lower, np.zeros_like(lower)]])


def pivot_table(planes, width_y, width_z, weight):
    cross = eigen_values(width_y)[:, None] + eigen_values(width_z)[None, :]
    diagonal = (1.0 + 2.0 * weight - weight * cross) / weight
    pivots = [1.0 / diagonal]
    for _ in range(planes // 2 - 1):
        pivots.append(1.0 / (diagonal - pivots[-1]))
    pivots.append(1.0 / (1.0 - pivots[-1] ** 2))
    return np.stack(pivots).astype(np.float32)


def ghost_table(across, steps):
    count, _, width = across.shape
    parts = two_parts(across)
    out = np.zeros((2, count, steps, 2, steps, 2, width), ml_dtypes.bfloat16)
    for n in range(steps):
        out[0, :, n, :, n, 0] = parts[0]
        out[0, :, n, :, n, 1] = parts[0]
        out[1, :, n, :, n, 0] = parts[1]
    return out.reshape(2 * count * steps * 2, steps * 2 * width)


def kick_table(across, steps):
    count, _, width = across.shape
    out = np.zeros((steps, width, 3, count, steps, 2), ml_dtypes.bfloat16)
    upper, lower = (np.transpose(a, (2, 0, 1)) for a in two_parts(across))
    for n in range(steps):
        for i, part in enumerate((upper, upper, lower)):
            out[n, :, i, :, n, :] = part
    return out.reshape(steps * width, 3 * count * steps * 2)


def split(values):
    upper = values.astype(jnp.bfloat16)
    return upper, (values - upper.astype(jnp.float32)).astype(jnp.bfloat16)


def times_right(values, table):
    width = values.shape[-1]
    both = jnp.dot(
        jnp.concatenate(split(values), axis=1), table, preferred_element_type=jnp.float32
    )
    return both[:, :width] + both[:, width:]


def times_left(table, *values):
    both = jnp.dot(
        table,
        jnp.concatenate([part for value in values for part in split(value)], axis=0),
        preferred_element_type=jnp.float32,
    )
    width = both.shape[0] // 2
    return both[:width] + both[width:]


def rates(spectrum):
    inverse = 1.0 / (1.0 - half * spectrum)
    return half * inverse, (1.0 + half * spectrum) * inverse


def side_by_side(count):
    return 2 if count % 2 == 0 else 1


def modal_kernel(
    arrived_ref, before_ref, guess_ref, spectrum_ref, x_ref, kick_ref, ghost_ref, *out_refs
):
    value_ref, second_ref, beyond_ref = out_refs
    n_space = arrived_ref.shape[0]
    own, width_x, width_z = before_ref.shape
    steps = beyond_ref.shape[2] // 2
    planes = width_x // n_space
    interval = pl.program_id(0)
    step = side_by_side(own)
    for first in range(0, own, step):
        each = range(first, first + step)

        def lines(begin, count):
            rows = [
                [arrived_ref[s, pl.ds(begin * own + q, count, stride=own), :] for q in each]
                for s in range(n_space)
            ]
            return [jnp.concatenate(row, axis=1) for row in rows]

        edges = lines(planes, 2 * steps)
        total = times_left(x_ref[...], jnp.concatenate(lines(0, planes), axis=0))
        upper, lower = split(jnp.concatenate(edges, axis=0))
        kicks = jnp.dot(
            kick_ref[...],
            jnp.concatenate([upper, lower, upper], axis=0),
            preferred_element_type=jnp.float32,
        )
        wide = lambda pieces: jnp.concatenate(list(pieces), axis=1)
        factor, fine = rates(wide(spectrum_ref[q] for q in each))
        drift, both = None, []
        for n in range(steps):
            kick = kicks[n * width_x : (n + 1) * width_x] * factor
            fresh = kick if drift is None else fine * drift + kick
            both.append(fresh if drift is None else fresh + drift)
            drift = fresh
        total = total + drift
        leap = (fine * fine) * (fine * fine) if steps == 4 else fine**steps
        guess = wide(guess_ref[q] for q in each)
        start = jnp.where(interval == 0, wide(before_ref[q] for q in each), guess)
        total = total + leap * start
        beyond = times_left(ghost_ref[...], *both)
        left = lax.broadcasted_iota(jnp.int32, edges[0].shape, 0) % 2 == 0
        blank = jnp.zeros_like(edges[0])
        for i, q in enumerate(each):
            lanes = slice(i * width_z, (i + 1) * width_z)
            value_ref[q] = total[:, lanes]
        for s in range(n_space):
            behind = pltpu.roll(edges[s - 1], 2 * steps - 1, 0) if s > 0 else blank
            ahead = pltpu.roll(edges[s + 1], 1, 0) if s < n_space - 1 else blank
            seen = beyond[s * 2 * steps : (s + 1) * 2 * steps] + jnp.where(left, behind, ahead)
            for i, q in enumerate(each):
                beyond_ref[q, s] = seen[:, i * width_z : (i + 1) * width_z]

        @pl.when(interval == 0)
        def _():
            second = leap * (total - guess)
            for i, q in enumerate(each):
                second_ref[q] = second[:, i * width_z : (i + 1) * width_z]


def modal(arrived, before, guess, spectrum, tables):
    n_space, _, total, own, width_z = arrived.shape
    width_x = before.shape[1]
    steps = (total - width_x // n_space) // 2
    still = lambda a: pl.BlockSpec(a.shape, lambda b: (0,) * a.ndim)
    lead = pl.BlockSpec((None, own, width_x, width_z), lambda b: (b, 0, 0, 0))
    return pl.pallas_call(
        modal_kernel,
        grid=(2,),
        out_shape=(
            jax.ShapeDtypeStruct((2, own, width_x, width_z), jnp.float32),
            jax.ShapeDtypeStruct((own, width_x, width_z), jnp.float32),
            jax.ShapeDtypeStruct((2, own, n_space, 2 * steps, width_z), jnp.float32),
        ),
        in_specs=[
            pl.BlockSpec((n_space, None, total * own, width_z), lambda b: (0, b, 0, 0)),
            still(before),
            pl.BlockSpec((None, own, width_x, width_z), lambda b: (0, 0, 0, 0)),
            still(spectrum),
            *(still(a) for a in tables),
        ],
        out_specs=(
            lead,
            still(before),
            pl.BlockSpec((None, own, n_space, 2 * steps, width_z), lambda b: (b, 0, 0, 0, 0)),
        ),
        cost_estimate=cost(arrived, before),
        compiler_params=room(40),
    )(arrived.reshape(n_space, 2, total * own, width_z), before, guess, spectrum, *tables)


def cells_kernel(wide_weight, lasts, spectrum_ref, x_ref, ghost_ref, *refs):
    *start_refs, out_ref = refs
    even_refs, start_refs = start_refs[:lasts], start_refs[lasts:]
    n_space = out_ref.shape[0]
    own, width_x, width_z = spectrum_ref.shape
    planes = width_x // n_space
    count = out_ref.shape[1] // own - planes
    steps = count // 2
    interval = pl.program_id(0)
    step = side_by_side(own)
    rows = own // lasts
    for first in range(0, own, step):
        each = range(first, first + step)
        wide = lambda pieces: jnp.concatenate(list(pieces), axis=1)
        spectrum = wide(spectrum_ref[q] for q in each)
        _, fine = rates(spectrum)
        even = wide(even_refs[q // rows][q % rows] for q in each)
        odd = wide(start_refs[0][q] for q in each)
        if wide_weight is not None:
            coarse = (1.0 + wide_weight * spectrum) / (1.0 - wide_weight * spectrum)
            odd = odd + coarse * even
        field = jnp.where(interval == 0, even, odd)
        both, power = [], field
        for n in range(steps if wide_weight is None else steps - 1):
            later = fine * power
            both.append(later + power)
            power = later
        if wide_weight is not None:
            both.append((coarse + 1.0) * field)
        total = times_left(x_ref[...], field)
        beyond = times_left(ghost_ref[...], *both)
        for i, q in enumerate(each):
            lanes = slice(i * width_z, (i + 1) * width_z)
            for s in range(n_space):
                seen = beyond[s * count : (s + 1) * count, lanes]
                if wide_weight is None:
                    seen = seen + start_refs[1][q, s]
                out_ref[s, pl.ds(q, planes, stride=own), :] = total[
                    s * planes : (s + 1) * planes, lanes
                ]
                out_ref[s, pl.ds(planes * own + q, count, stride=own), :] = seen


def to_cells(wide_weight, spectrum, tables, n_space, steps, evens, others):
    own, width_x, width_z = spectrum.shape
    planes = width_x // n_space
    total = planes + 2 * steps
    still = lambda a: pl.BlockSpec(a.shape, lambda b: (0,) * a.ndim)

    def placed(array):
        if array.shape[0] == 2 and array.ndim > 3:
            tail = array.shape[1:]
            pick = (lambda b: (0,) + (0,) * len(tail)) if array.ndim == 4 else (
                lambda b: (b,) + (0,) * len(tail)
            )
            return pl.BlockSpec((None, *tail), pick)
        return still(array)

    out = pl.pallas_call(
        lambda *refs: cells_kernel(wide_weight, len(evens), *refs),
        grid=(2,),
        out_shape=jax.ShapeDtypeStruct((n_space, 2, total * own, width_z), jnp.float32),
        in_specs=[
            still(spectrum),
            *(still(a) for a in tables),
            *(still(a) for a in evens),
            *(placed(a) for a in others),
        ],
        out_specs=pl.BlockSpec((n_space, None, total * own, width_z), lambda b: (0, b, 0, 0)),
        cost_estimate=cost(spectrum, spectrum),
        compiler_params=room(40),
    )(spectrum, *tables, *evens, *others)
    return out.reshape(2 * n_space, total, own, width_z)


def solve(planes, right, pivot, work, left_ghost, right_ghost, finish):
    middle = planes // 2
    lower, upper = left_ghost, right_ghost
    for k in range(middle):
        low, top = right(k), right(planes - 1 - k)
        low = low if lower is None else low + lower
        top = top if upper is None else top + upper
        factor = pivot(k)
        lower, upper = low * factor, top * factor
        if k < middle - 1:
            work[k] = lower
            work[planes - 1 - k] = upper
    factor, joint = pivot(middle - 1), pivot(middle)
    lower, upper = (lower + factor * upper) * joint, (upper + factor * lower) * joint
    finish(middle - 1, lower)
    finish(planes - middle, upper)
    for k in range(middle - 2, -1, -1):
        factor = pivot(k)
        lower = work[k] + factor * lower
        upper = work[planes - 1 - k] + factor * upper
        finish(k, lower)
        finish(planes - 1 - k, upper)


def transformed(block, z_ref, y_ref):
    count, width_y, width_z = block.shape
    lines = times_right(block.reshape(count * width_y, width_z), z_ref[...])
    step = 2 if count % 2 == 0 else 1
    out = []
    for i in range(0, count, step):
        wide = [lines[(i + j) * width_y : (i + j + 1) * width_y] for j in range(step)]
        wide = times_left(y_ref[...], jnp.concatenate(wide, axis=1))
        out += [wide[:, j * width_z : (j + 1) * width_z] for j in range(step)]
    return out


def front_kernel(x_steps, forcing_ref, z_ref, y_ref, pivot_ref, pushed_ref, out_ref, kept, work):
    steps, count, width_y, width_z = forcing_ref.shape
    planes, parts, own = kept.shape[1:4]
    some = out_ref.shape[0]
    turn = pl.program_id(0)

    @pl.when(turn < x_steps)
    def _():
        for n in range(steps):
            for i, plane in enumerate(transformed(forcing_ref[n], z_ref, y_ref)):
                pushed_ref[n, i] = plane
                kept[n, turn * count + i] = plane.reshape(parts, own, width_z)

    @pl.when(turn >= x_steps)
    def _():
        place = pl.ds((turn - x_steps) * some, some)
        for n in range(steps):

            def right(k):
                pushed = kept[n, k, place]
                return pushed if n == 0 else pushed + (2.0 / half) * out_ref[:, k]

            def finish(k, solved):
                if k == 0:
                    out_ref[:, planes + 2 * n] = solved
                if k == planes - 1:
                    out_ref[:, planes + 2 * n + 1] = solved
                out_ref[:, k] = solved if n == 0 else solved - out_ref[:, k]

            solve(planes, right, lambda k: pivot_ref[k], work, None, None, finish)


def front(forcing, z_right, y_left, pivots, parts):
    steps, planes, width_y, width_z = forcing.shape
    own = width_y // parts
    count = 4 if planes % 4 == 0 else 1
    some = 2 if parts % 2 == 0 else 1
    x_steps, q_steps = planes // count, parts // some
    early = lambda i: jnp.minimum(i, x_steps - 1)
    late = lambda i: jnp.maximum(i - x_steps, 0)
    total = planes + 2 * steps
    return pl.pallas_call(
        lambda *refs: front_kernel(x_steps, *refs),
        grid=(x_steps + q_steps,),
        out_shape=(
            jax.ShapeDtypeStruct(forcing.shape, jnp.float32),
            jax.ShapeDtypeStruct((parts, total, own, width_z), jnp.float32),
        ),
        in_specs=[
            pl.BlockSpec((steps, count, width_y, width_z), lambda i: (0, early(i), 0, 0)),
            pl.BlockSpec(z_right.shape, lambda i: (0, 0)),
            pl.BlockSpec(y_left.shape, lambda i: (0, 0)),
            pl.BlockSpec((planes // 2 + 1, some, own, width_z), lambda i: (0, late(i), 0, 0)),
        ],
        out_specs=(
            pl.BlockSpec((steps, count, width_y, width_z), lambda i: (0, early(i), 0, 0)),
            pl.BlockSpec((some, total, own, width_z), lambda i: (late(i), 0, 0, 0)),
        ),
        scratch_shapes=[
            pltpu.VMEM((steps, planes, parts, own, width_z), jnp.float32),
            pltpu.VMEM((planes, some, own, width_z), jnp.float32),
        ],
        cost_estimate=cost(forcing),
        compiler_params=room(24),
    )(forcing, z_right, y_left, pivots)


def opening_kernel(g_steps, pair_ref, guess_ref, initial_ref, z_ref, y_ref, out_ref):
    parts, count, own, width_z = out_ref.shape
    block = jnp.where(pl.program_id(0) < g_steps, guess_ref[...], initial_ref[...])
    for i, plane in enumerate(transformed(block, z_ref, y_ref)):
        out_ref[:, i] = plane.reshape(parts, own, width_z)


def opening_fields(guess, initial, z_right, y_left, pair, parts):
    planes, width_y, width_z = guess.shape
    share = planes // 2
    count = next(c for c in (16, 8, 1) if share % c == 0)
    g_steps, a_steps = planes // count, share // count
    own = width_y // parts
    block = (count, width_y, width_z)
    whole = lambda a: pl.BlockSpec(a.shape, lambda i, p: (0, 0))
    return pl.pallas_call(
        lambda *refs: opening_kernel(g_steps, *refs),
        grid_spec=pltpu.PrefetchScalarGridSpec(
            num_scalar_prefetch=1,
            grid=(g_steps + a_steps,),
            in_specs=[
                pl.BlockSpec(block, lambda i, p: (jnp.minimum(i, g_steps - 1), 0, 0)),
                pl.BlockSpec(
                    block, lambda i, p: (p[0] * a_steps + jnp.maximum(i - g_steps, 0), 0, 0)
                ),
                whole(z_right),
                whole(y_left),
            ],
            out_specs=pl.BlockSpec((parts, count, own, width_z), lambda i, p: (0, i, 0, 0)),
        ),
        out_shape=jax.ShapeDtypeStruct((parts, planes + share, own, width_z), jnp.float32),
        cost_estimate=cost(guess),
        compiler_params=room(60),
    )(pair[None], guess, initial, z_right, y_left)


def relax_kernel(pushed_ref, early_ref, fine_ref, out_ref, work):
    steps, planes = out_ref.shape[:2]
    for n in range(steps):

        def old(k):
            return early_ref[:, k] if n == 0 else out_ref[n - 1, k]

        def right(k):
            return pushed_ref[n, k] + (2.0 / half) * old(k)

        def keep(k, solved):
            out_ref[n, k] = solved - old(k)

        ghosts = [early_ref[:, planes + 2 * n + i] for i in (0, 1)]
        solve(planes, right, lambda k: fine_ref[k], work, *ghosts, keep)


def relax(pushed, early, fine_pivots):
    steps, planes, parts, own, width_z = pushed.shape
    step = 2 if parts % 2 == 0 else 1
    block = pl.BlockSpec((steps, planes, step, own, width_z), lambda i: (0, 0, i, 0, 0))
    return pl.pallas_call(
        relax_kernel,
        grid=(parts // step,),
        out_shape=jax.ShapeDtypeStruct(pushed.shape, jnp.float32),
        in_specs=[
            block,
            pl.BlockSpec((step, early.shape[1], own, width_z), lambda i: (i, 0, 0, 0)),
            pl.BlockSpec((planes // 2 + 1, step, own, width_z), lambda i: (0, i, 0, 0)),
        ],
        out_specs=block,
        scratch_shapes=[pltpu.VMEM((planes, step, own, width_z), jnp.float32)],
        cost_estimate=cost(early),
        compiler_params=room(60),
    )(pushed, early, fine_pivots)


def finish_kernel(q_steps, relaxed_ref, *refs):
    *late_refs, fine_ref, wide_ref, y_ref, z_ref, out_ref, points, state, work = refs
    steps, count, width_y, width_z = out_ref.shape
    planes = points.shape[1]
    some = state.shape[1]
    wide = steps * half
    turn = pl.program_id(0)

    def late(k):
        return jnp.concatenate([ref[:, k] for ref in late_refs], axis=1)

    @pl.when(turn < q_steps)
    def _():
        place = pl.ds(turn * some, some)

        def sent(k, solved):
            points[steps - 1, k, place] = relaxed_ref[steps - 1, k] + (solved - late(k))

        ghosts = [late(planes + 2 * (steps - 1) + i) for i in (0, 1)]
        solve(planes, lambda k: (2.0 / wide) * late(k), lambda k: wide_ref[k], work, *ghosts, sent)
        for n in range(steps - 1):

            def old(k):
                return late(k) if n == 0 else state[k]

            def right(k):
                return (2.0 / half) * old(k)

            def keep(k, solved):
                fresh = solved - old(k)
                state[k] = fresh
                points[n, k, place] = relaxed_ref[n, k] + fresh

            ghosts = [late(planes + 2 * n + i) for i in (0, 1)]
            solve(planes, right, lambda k: fine_ref[k], work, *ghosts, keep)

    @pl.when(turn >= q_steps)
    def _():
        first = (turn - q_steps) * count
        step = 2 if count % 2 == 0 else 1
        for n in range(steps):
            lines = []
            for i in range(0, count, step):
                wide = [points[n, first + i + j].reshape(width_y, width_z) for j in range(step)]
                wide = times_left(y_ref[...], jnp.concatenate(wide, axis=1))
                lines += [wide[:, j * width_z : (j + 1) * width_z] for j in range(step)]
            block = times_right(jnp.concatenate(lines, axis=0), z_ref[...])
            out_ref[n] = block.reshape(count, width_y, width_z)


def finish(relaxed, lates, fine_pivots, wide_pivots, y_left, z_right):
    steps, planes, parts, own, width_z = relaxed.shape
    width_y = parts * own
    some = 2 if parts % 2 == 0 else 1
    count = 4 if planes % 4 == 0 else 1
    q_steps, x_steps = parts // some, planes // count
    ahead = lambda i: jnp.minimum(i, q_steps - 1)
    after = lambda i: jnp.maximum(i - q_steps, 0)
    pivots = pl.BlockSpec((planes // 2 + 1, some, own, width_z), lambda i: (0, ahead(i), 0, 0))
    return pl.pallas_call(
        lambda *refs: finish_kernel(q_steps, *refs),
        grid=(q_steps + x_steps,),
        out_shape=jax.ShapeDtypeStruct((steps, planes, width_y, width_z), jnp.float32),
        in_specs=[
            pl.BlockSpec((steps, planes, some, own, width_z), lambda i: (0, 0, ahead(i), 0, 0)),
            *(
                pl.BlockSpec((some, *late.shape[1:]), lambda i: (ahead(i), 0, 0, 0))
                for late in lates
            ),
            pivots,
            pivots,
            pl.BlockSpec(y_left.shape, lambda i: (0, 0)),
            pl.BlockSpec(z_right.shape, lambda i: (0, 0)),
        ],
        out_specs=pl.BlockSpec((steps, count, width_y, width_z), lambda i: (0, after(i), 0, 0)),
        scratch_shapes=[
            pltpu.VMEM(relaxed.shape, jnp.float32),
            pltpu.VMEM((planes, some, own, width_z), jnp.float32),
            pltpu.VMEM((planes, some, own, width_z), jnp.float32),
        ],
        cost_estimate=cost(relaxed),
        compiler_params=room(60),
    )(relaxed, *lates, fine_pivots, wide_pivots, y_left, z_right)


def per_device(forcing, coarse_guess, initial):
    steps, planes, width_y, width_z = forcing.shape
    n_space = lax.axis_size("space")
    n_plane = lax.axis_size("plane")
    width_x = planes * n_space
    parts = 2 * n_space
    own = width_y // parts
    chunks = 2 if own % 16 == 0 else 1
    rows = own // chunks
    table_x = jnp.asarray(sine_table(width_x))
    z_right = jnp.asarray(right_table(sine_table(width_z)))
    y_left = jnp.asarray(left_table(sine_table(width_y)))
    y_scaled = jnp.asarray(left_table((time_step / half) * sine_table(width_y)))
    fine_pivots = pivot_table(planes, width_y, width_z, half)
    wide_pivots = pivot_table(planes, width_y, width_z, steps * half)
    pair = lax.axis_index("pair")
    level = lax.axis_index("plane")
    offset = (lax.axis_index("space") * 2 + pair) * own
    e_x, e_y, e_z = (
        jnp.asarray(eigen_values(n).astype(np.float32)) for n in (width_x, width_y, width_z)
    )
    spectrum = (
        e_x[None, :, None]
        + lax.dynamic_slice_in_dim(e_y, offset, own)[:, None, None]
        + e_z[None, None, :]
    )
    fine = (1.0 + half * spectrum) / (1.0 - half * spectrum)
    wide = steps * half
    coarse = (1.0 + wide * spectrum) / (1.0 - wide * spectrum)
    leap = fine
    for _ in range(steps - 1):
        leap = leap * fine

    def swap(fields):
        return lax.all_to_all(fields, ("space", "pair"), split_axis=0, concat_axis=0, tiled=True)

    def spread(fields):
        return swap(fields).reshape(n_space, 2, *fields.shape[1:])

    by_device = table_x.reshape(n_space, planes, width_x)

    def modes(cells):
        return jnp.einsum("sbmqr,smp->bqpr", cells, by_device, precision=high)

    share = planes // 2
    opened = opening_fields(coarse_guess[0], initial, z_right, y_left, pair, parts)
    opened, forcing = lax.optimization_barrier((opened, forcing))
    opened = spread(opened)
    pushed, relaxed = front(
        forcing, z_right, y_scaled, jnp.asarray(fine_pivots.reshape(-1, parts, own, width_z)), parts
    )
    opened, relaxed = lax.optimization_barrier((opened, relaxed))
    arrived = spread(relaxed)

    guess = modes(opened[:, :, :planes])
    before = lax.ppermute(guess[1], "plane", [(i, (i + 1) % n_plane) for i in range(n_plane)])
    anchor = jnp.einsum(
        "sbmqr,sbmp->qpr",
        opened[:, :, planes:],
        table_x.reshape(n_space, 2, share, width_x),
        precision=high,
    )

    full = np.concatenate([np.zeros((1, width_x)), sine_table(width_x), np.zeros((1, width_x))])
    across = np.stack([full[0:width_x:planes], full[planes + 1 :: planes]], axis=1)
    across = across.astype(np.float32)
    x_left = jnp.asarray(left_table(sine_table(width_x)))
    ghost_left = jnp.asarray(ghost_table(across, steps))
    kick_left = jnp.asarray(kick_table(across, steps))
    value, second_residual, beyond = modal(
        arrived, before, guess, spectrum, (x_left, kick_left, ghost_left)
    )

    def chunk_of(array, c):
        return lax.slice_in_dim(array, c * rows, (c + 1) * rows, axis=0)

    shifted = [
        lax.ppermute(chunk_of(value[1], c), "plane", [(i, i + 1) for i in range(n_plane - 1)])
        for c in range(chunks)
    ]
    rate = [chunk_of(coarse, c) for c in range(chunks)]
    second = [chunk_of(second_residual, c) for c in range(chunks)]
    start = [chunk_of(before, c) for c in range(chunks)]
    carries = [jnp.zeros_like(start[0])] * chunks
    lasts, firsts, sent = [], [], []

    def onward(c, carried):
        return rate[c] * (rate[c] * carried + firsts[c]) + second[c]

    def hop(c, sent, place):
        return lax.ppermute(sent, "plane", [(place, place + 1)])

    swapped = []
    for c in range(chunks):
        if c > 0:
            sent[c - 1], start[c] = lax.optimization_barrier((sent[c - 1], start[c]))
        lasts.append(jnp.where(level == 0, chunk_of(anchor, c), shifted[c]))
        firsts.append(chunk_of(leap, c) * (lasts[c] - start[c]))
        sent.append(onward(c, carries[c]))
        other = jnp.where(pair == 0, second[c], firsts[c])
        swapped.append(lax.ppermute(other, "pair", [(0, 1), (1, 0)]))
    carries[0] = carries[0] + hop(0, sent[0], 0)
    following = onward(0, carries[0])
    following, lasts, swapped = lax.optimization_barrier((following, lasts, swapped))
    tables = (x_left, ghost_left)
    early = swap(to_cells(None, spectrum, tables, n_space, steps, lasts, (value, beyond)))
    for place in range(n_plane - 1):
        for c in range(chunks):
            if place > 0:
                sent[c] = following if place + c == 1 else onward(c, carries[c])
            if c < chunks - 1:
                sent[c], second[c + 1] = lax.optimization_barrier((sent[c], second[c + 1]))
            if c == chunks - 1 and place == n_plane - 2:
                sent[c], pushed = lax.optimization_barrier((sent[c], pushed))
            if place + c > 0:
                carries[c] = carries[c] + hop(c, sent[c], place)
    mine = jnp.where(pair == 0, jnp.concatenate(firsts, axis=0), second_residual)
    other = jnp.concatenate(swapped, axis=0)
    fine_pivots, wide_pivots = (
        jnp.asarray(a.reshape(-1, parts, own, width_z)) for a in (fine_pivots, wide_pivots)
    )
    relaxed = relax(pushed.reshape(steps, planes, parts, own, width_z), early, fine_pivots)
    firsts, relaxed = lax.optimization_barrier((firsts, relaxed))
    lates = []
    for c in range(chunks):
        late = to_cells(
            wide, chunk_of(spectrum, c), tables, n_space, steps, carries[c : c + 1], (firsts[c],)
        )
        late, relaxed, mine = lax.optimization_barrier((late, relaxed, mine))
        lates.append(swap(late))
    residual = jnp.concatenate(
        [jnp.where(pair == 0, mine, other), jnp.where(pair == 0, other, mine)], axis=0
    ).transpose(1, 0, 2)
    points = finish(relaxed, lates, fine_pivots, wide_pivots, y_left, z_right)
    return (points, residual[None])


def solution(mesh):
    whole = mesh.devices
    cut = Mesh(whole.reshape(whole.shape[0] // 2, 2, whole.shape[1]), ("plane", "pair", "space"))
    both = ("plane", "pair")
    placed = (P(both, "space", None, None), P(both, "space", None, None), P("space", None, None))
    return jax.shard_map(
        per_device,
        mesh=cut,
        in_specs=placed,
        out_specs=(P(both, "space", None, None), P(both, None, "space", None)),
        check_vma=False,
    )
```

```python
import jax
import jax.numpy as jnp
import ml_dtypes
import numpy as np
from jax import lax
from jax.experimental import pallas as pl
from jax.experimental.pallas import tpu as pltpu
from jax.sharding import Mesh
from jax.sharding import PartitionSpec as P

time_step = 0.5
half = 0.5 * time_step
high = lax.Precision.HIGH


def room(mebibytes):
    return pltpu.CompilerParams(vmem_limit_bytes=mebibytes << 20)


def cost(*arrays):
    moved = sum(int(np.prod(a.shape)) * 4 for a in arrays)
    return pl.CostEstimate(flops=moved * 400, bytes_accessed=2 * moved, transcendentals=0)


def sine_table(length):
    ladder = np.arange(1, length + 1, dtype=np.float64)
    table = np.sqrt(2.0 / (length + 1)) * np.sin(
        np.pi * ladder[:, None] * ladder[None, :] / (length + 1)
    )
    return table.astype(np.float32)


def eigen_values(length):
    ladder = np.arange(1, length + 1, dtype=np.float64)
    return -4.0 * np.sin(np.pi * ladder / (2 * (length + 1))) ** 2


def two_parts(table):
    upper = table.astype(ml_dtypes.bfloat16)
    return upper, (table - upper.astype(np.float32)).astype(ml_dtypes.bfloat16)


def right_table(table):
    upper, lower = two_parts(table)
    return np.block([[upper, lower], [upper, np.zeros_like(lower)]])


def left_table(table):
    upper, lower = two_parts(table)
    return np.block([[upper, upper], [lower, np.zeros_like(lower)]])


def pivot_table(planes, width_y, width_z, weight):
    cross = eigen_values(width_y)[:, None] + eigen_values(width_z)[None, :]
    diagonal = (1.0 + 2.0 * weight - weight * cross) / weight
    pivots = [1.0 / diagonal]
    for _ in range(planes // 2 - 1):
        pivots.append(1.0 / (diagonal - pivots[-1]))
    pivots.append(1.0 / (1.0 - pivots[-1] ** 2))
    return np.stack(pivots).astype(np.float32)


def ghost_table(across, steps):
    count, _, width = across.shape
    parts = two_parts(across)
    out = np.zeros((2, count, steps, 2, steps, 2, width), ml_dtypes.bfloat16)
    for n in range(steps):
        out[0, :, n, :, n, 0] = parts[0]
        out[0, :, n, :, n, 1] = parts[0]
        out[1, :, n, :, n, 0] = parts[1]
    return out.reshape(2 * count * steps * 2, steps * 2 * width)


def kick_table(across, steps):
    count, _, width = across.shape
    out = np.zeros((steps, width, 3, count, steps, 2), ml_dtypes.bfloat16)
    upper, lower = (np.transpose(a, (2, 0, 1)) for a in two_parts(across))
    for n in range(steps):
        for i, part in enumerate((upper, upper, lower)):
            out[n, :, i, :, n, :] = part
    return out.reshape(steps * width, 3 * count * steps * 2)


def split(values):
    upper = values.astype(jnp.bfloat16)
    return upper, (values - upper.astype(jnp.float32)).astype(jnp.bfloat16)


def times_right(values, table):
    width = values.shape[-1]
    both = jnp.dot(
        jnp.concatenate(split(values), axis=1), table, preferred_element_type=jnp.float32
    )
    return both[:, :width] + both[:, width:]


def times_left(table, *values):
    both = jnp.dot(
        table,
        jnp.concatenate([part for value in values for part in split(value)], axis=0),
        preferred_element_type=jnp.float32,
    )
    width = both.shape[0] // 2
    return both[:width] + both[width:]


def rates(spectrum):
    inverse = 1.0 / (1.0 - half * spectrum)
    return half * inverse, (1.0 + half * spectrum) * inverse


def side_by_side(count):
    return 2 if count % 2 == 0 else 1


def modal_kernel(
    arrived_ref, before_ref, guess_ref, spectrum_ref, x_ref, kick_ref, ghost_ref, *out_refs
):
    value_ref, second_ref, beyond_ref = out_refs
    n_space = arrived_ref.shape[0]
    own, width_x, width_z = before_ref.shape
    steps = beyond_ref.shape[2] // 2
    planes = width_x // n_space
    interval = pl.program_id(0)
    step = side_by_side(own)
    for first in range(0, own, step):
        each = range(first, first + step)

        def lines(begin, count):
            rows = [
                [arrived_ref[s, pl.ds(begin * own + q, count, stride=own), :] for q in each]
                for s in range(n_space)
            ]
            return [jnp.concatenate(row, axis=1) for row in rows]

        edges = lines(planes, 2 * steps)
        total = times_left(x_ref[...], jnp.concatenate(lines(0, planes), axis=0))
        upper, lower = split(jnp.concatenate(edges, axis=0))
        kicks = jnp.dot(
            kick_ref[...],
            jnp.concatenate([upper, lower, upper], axis=0),
            preferred_element_type=jnp.float32,
        )
        wide = lambda pieces: jnp.concatenate(list(pieces), axis=1)
        factor, fine = rates(wide(spectrum_ref[q] for q in each))
        drift, both = None, []
        for n in range(steps):
            kick = kicks[n * width_x : (n + 1) * width_x] * factor
            fresh = kick if drift is None else fine * drift + kick
            both.append(fresh if drift is None else fresh + drift)
            drift = fresh
        total = total + drift
        leap = (fine * fine) * (fine * fine) if steps == 4 else fine**steps
        guess = wide(guess_ref[q] for q in each)
        start = jnp.where(interval == 0, wide(before_ref[q] for q in each), guess)
        total = total + leap * start
        beyond = times_left(ghost_ref[...], *both)
        left = lax.broadcasted_iota(jnp.int32, edges[0].shape, 0) % 2 == 0
        blank = jnp.zeros_like(edges[0])
        for i, q in enumerate(each):
            lanes = slice(i * width_z, (i + 1) * width_z)
            value_ref[q] = total[:, lanes]
        for s in range(n_space):
            behind = pltpu.roll(edges[s - 1], 2 * steps - 1, 0) if s > 0 else blank
            ahead = pltpu.roll(edges[s + 1], 1, 0) if s < n_space - 1 else blank
            seen = beyond[s * 2 * steps : (s + 1) * 2 * steps] + jnp.where(left, behind, ahead)
            for i, q in enumerate(each):
                beyond_ref[q, s] = seen[:, i * width_z : (i + 1) * width_z]

        @pl.when(interval == 0)
        def _():
            second = leap * (total - guess)
            for i, q in enumerate(each):
                second_ref[q] = second[:, i * width_z : (i + 1) * width_z]


def modal(arrived, before, guess, spectrum, tables):
    n_space, _, total, own, width_z = arrived.shape
    width_x = before.shape[1]
    steps = (total - width_x // n_space) // 2
    still = lambda a: pl.BlockSpec(a.shape, lambda b: (0,) * a.ndim)
    lead = pl.BlockSpec((None, own, width_x, width_z), lambda b: (b, 0, 0, 0))
    return pl.pallas_call(
        modal_kernel,
        grid=(2,),
        out_shape=(
            jax.ShapeDtypeStruct((2, own, width_x, width_z), jnp.float32),
            jax.ShapeDtypeStruct((own, width_x, width_z), jnp.float32),
            jax.ShapeDtypeStruct((2, own, n_space, 2 * steps, width_z), jnp.float32),
        ),
        in_specs=[
            pl.BlockSpec((n_space, None, total * own, width_z), lambda b: (0, b, 0, 0)),
            still(before),
            pl.BlockSpec((None, own, width_x, width_z), lambda b: (0, 0, 0, 0)),
            still(spectrum),
            *(still(a) for a in tables),
        ],
        out_specs=(
            lead,
            still(before),
            pl.BlockSpec((None, own, n_space, 2 * steps, width_z), lambda b: (b, 0, 0, 0, 0)),
        ),
        cost_estimate=cost(arrived, before),
        compiler_params=room(40),
    )(arrived.reshape(n_space, 2, total * own, width_z), before, guess, spectrum, *tables)


def cells_kernel(wide_weight, lasts, spectrum_ref, x_ref, ghost_ref, *refs):
    *start_refs, out_ref = refs
    even_refs, start_refs = start_refs[:lasts], start_refs[lasts:]
    n_space = out_ref.shape[0]
    own, width_x, width_z = spectrum_ref.shape
    planes = width_x // n_space
    count = out_ref.shape[1] // own - planes
    steps = count // 2
    interval = pl.program_id(0)
    step = side_by_side(own)
    rows = own // lasts
    for first in range(0, own, step):
        each = range(first, first + step)
        wide = lambda pieces: jnp.concatenate(list(pieces), axis=1)
        spectrum = wide(spectrum_ref[q] for q in each)
        _, fine = rates(spectrum)
        even = wide(even_refs[q // rows][q % rows] for q in each)
        odd = wide(start_refs[0][q] for q in each)
        if wide_weight is not None:
            coarse = (1.0 + wide_weight * spectrum) / (1.0 - wide_weight * spectrum)
            odd = odd + coarse * even
        field = jnp.where(interval == 0, even, odd)
        both, power = [], field
        for n in range(steps if wide_weight is None else steps - 1):
            later = fine * power
            both.append(later + power)
            power = later
        if wide_weight is not None:
            both.append((coarse + 1.0) * field)
        total = times_left(x_ref[...], field)
        beyond = times_left(ghost_ref[...], *both)
        for i, q in enumerate(each):
            lanes = slice(i * width_z, (i + 1) * width_z)
            for s in range(n_space):
                seen = beyond[s * count : (s + 1) * count, lanes]
                if wide_weight is None:
                    seen = seen + start_refs[1][q, s]
                out_ref[s, pl.ds(q, planes, stride=own), :] = total[
                    s * planes : (s + 1) * planes, lanes
                ]
                out_ref[s, pl.ds(planes * own + q, count, stride=own), :] = seen


def to_cells(wide_weight, spectrum, tables, n_space, steps, evens, others):
    own, width_x, width_z = spectrum.shape
    planes = width_x // n_space
    total = planes + 2 * steps
    still = lambda a: pl.BlockSpec(a.shape, lambda b: (0,) * a.ndim)

    def placed(array):
        if array.shape[0] == 2 and array.ndim > 3:
            tail = array.shape[1:]
            pick = (lambda b: (0,) + (0,) * len(tail)) if array.ndim == 4 else (
                lambda b: (b,) + (0,) * len(tail)
            )
            return pl.BlockSpec((None, *tail), pick)
        return still(array)

    out = pl.pallas_call(
        lambda *refs: cells_kernel(wide_weight, len(evens), *refs),
        grid=(2,),
        out_shape=jax.ShapeDtypeStruct((n_space, 2, total * own, width_z), jnp.float32),
        in_specs=[
            still(spectrum),
            *(still(a) for a in tables),
            *(still(a) for a in evens),
            *(placed(a) for a in others),
        ],
        out_specs=pl.BlockSpec((n_space, None, total * own, width_z), lambda b: (0, b, 0, 0)),
        cost_estimate=cost(spectrum, spectrum),
        compiler_params=room(40),
    )(spectrum, *tables, *evens, *others)
    return out.reshape(2 * n_space, total, own, width_z)


def solve(planes, right, pivot, work, left_ghost, right_ghost, finish):
    middle = planes // 2
    lower, upper = left_ghost, right_ghost
    for k in range(middle):
        low, top = right(k), right(planes - 1 - k)
        low = low if lower is None else low + lower
        top = top if upper is None else top + upper
        factor = pivot(k)
        lower, upper = low * factor, top * factor
        if k < middle - 1:
            work[k] = lower
            work[planes - 1 - k] = upper
    factor, joint = pivot(middle - 1), pivot(middle)
    lower, upper = (lower + factor * upper) * joint, (upper + factor * lower) * joint
    finish(middle - 1, lower)
    finish(planes - middle, upper)
    for k in range(middle - 2, -1, -1):
        factor = pivot(k)
        lower = work[k] + factor * lower
        upper = work[planes - 1 - k] + factor * upper
        finish(k, lower)
        finish(planes - 1 - k, upper)


def transformed(block, z_ref, y_ref):
    count, width_y, width_z = block.shape
    lines = times_right(block.reshape(count * width_y, width_z), z_ref[...])
    step = 2 if count % 2 == 0 else 1
    out = []
    for i in range(0, count, step):
        wide = [lines[(i + j) * width_y : (i + j + 1) * width_y] for j in range(step)]
        wide = times_left(y_ref[...], jnp.concatenate(wide, axis=1))
        out += [wide[:, j * width_z : (j + 1) * width_z] for j in range(step)]
    return out


def front_kernel(x_steps, forcing_ref, z_ref, y_ref, pivot_ref, pushed_ref, out_ref, kept, work):
    steps, count, width_y, width_z = forcing_ref.shape
    planes, parts, own = kept.shape[1:4]
    some = out_ref.shape[0]
    turn = pl.program_id(0)

    @pl.when(turn < x_steps)
    def _():
        for n in range(steps):
            for i, plane in enumerate(transformed(forcing_ref[n], z_ref, y_ref)):
                pushed_ref[n, i] = plane
                kept[n, turn * count + i] = plane.reshape(parts, own, width_z)

    @pl.when(turn >= x_steps)
    def _():
        place = pl.ds((turn - x_steps) * some, some)
        for n in range(steps):

            def right(k):
                pushed = kept[n, k, place]
                return pushed if n == 0 else pushed + (2.0 / half) * out_ref[:, k]

            def finish(k, solved):
                if k == 0:
                    out_ref[:, planes + 2 * n] = solved
                if k == planes - 1:
                    out_ref[:, planes + 2 * n + 1] = solved
                out_ref[:, k] = solved if n == 0 else solved - out_ref[:, k]

            solve(planes, right, lambda k: pivot_ref[k], work, None, None, finish)


def front(forcing, z_right, y_left, pivots, parts):
    steps, planes, width_y, width_z = forcing.shape
    own = width_y // parts
    count = 4 if planes % 4 == 0 else 1
    some = 2 if parts % 2 == 0 else 1
    x_steps, q_steps = planes // count, parts // some
    early = lambda i: jnp.minimum(i, x_steps - 1)
    late = lambda i: jnp.maximum(i - x_steps, 0)
    total = planes + 2 * steps
    return pl.pallas_call(
        lambda *refs: front_kernel(x_steps, *refs),
        grid=(x_steps + q_steps,),
        out_shape=(
            jax.ShapeDtypeStruct(forcing.shape, jnp.float32),
            jax.ShapeDtypeStruct((parts, total, own, width_z), jnp.float32),
        ),
        in_specs=[
            pl.BlockSpec((steps, count, width_y, width_z), lambda i: (0, early(i), 0, 0)),
            pl.BlockSpec(z_right.shape, lambda i: (0, 0)),
            pl.BlockSpec(y_left.shape, lambda i: (0, 0)),
            pl.BlockSpec((planes // 2 + 1, some, own, width_z), lambda i: (0, late(i), 0, 0)),
        ],
        out_specs=(
            pl.BlockSpec((steps, count, width_y, width_z), lambda i: (0, early(i), 0, 0)),
            pl.BlockSpec((some, total, own, width_z), lambda i: (late(i), 0, 0, 0)),
        ),
        scratch_shapes=[
            pltpu.VMEM((steps, planes, parts, own, width_z), jnp.float32),
            pltpu.VMEM((planes, some, own, width_z), jnp.float32),
        ],
        cost_estimate=cost(forcing),
        compiler_params=room(24),
    )(forcing, z_right, y_left, pivots)


def opening_kernel(g_steps, pair_ref, guess_ref, initial_ref, z_ref, y_ref, out_ref):
    parts, count, own, width_z = out_ref.shape
    block = jnp.where(pl.program_id(0) < g_steps, guess_ref[...], initial_ref[...])
    for i, plane in enumerate(transformed(block, z_ref, y_ref)):
        out_ref[:, i] = plane.reshape(parts, own, width_z)


def opening_fields(guess, initial, z_right, y_left, pair, parts):
    planes, width_y, width_z = guess.shape
    share = planes // 2
    count = next(c for c in (16, 8, 1) if share % c == 0)
    g_steps, a_steps = planes // count, share // count
    own = width_y // parts
    block = (count, width_y, width_z)
    whole = lambda a: pl.BlockSpec(a.shape, lambda i, p: (0, 0))
    return pl.pallas_call(
        lambda *refs: opening_kernel(g_steps, *refs),
        grid_spec=pltpu.PrefetchScalarGridSpec(
            num_scalar_prefetch=1,
            grid=(g_steps + a_steps,),
            in_specs=[
                pl.BlockSpec(block, lambda i, p: (jnp.minimum(i, g_steps - 1), 0, 0)),
                pl.BlockSpec(
                    block, lambda i, p: (p[0] * a_steps + jnp.maximum(i - g_steps, 0), 0, 0)
                ),
                whole(z_right),
                whole(y_left),
            ],
            out_specs=pl.BlockSpec((parts, count, own, width_z), lambda i, p: (0, i, 0, 0)),
        ),
        out_shape=jax.ShapeDtypeStruct((parts, planes + share, own, width_z), jnp.float32),
        cost_estimate=cost(guess),
        compiler_params=room(60),
    )(pair[None], guess, initial, z_right, y_left)


def finish_kernel(q_steps, pushed_ref, early_ref, *refs):
    *late_refs, fine_ref, wide_ref, y_ref, z_ref, out_ref, points, state, work = refs
    steps, count, width_y, width_z = out_ref.shape
    planes = points.shape[1]
    some = state.shape[1]
    wide = steps * half
    turn = pl.program_id(0)

    def late(k):
        return jnp.concatenate([ref[:, k] for ref in late_refs], axis=1)

    @pl.when(turn < q_steps)
    def _():
        place = pl.ds(turn * some, some)
        for n in range(steps):

            def old(k):
                return early_ref[:, k] if n == 0 else points[n - 1, k, place]

            def right(k):
                return pushed_ref[n, k] + (2.0 / half) * old(k)

            def keep(k, solved):
                points[n, k, place] = solved - old(k)

            ghosts = [early_ref[:, planes + 2 * n + i] for i in (0, 1)]
            solve(planes, right, lambda k: fine_ref[k], work, *ghosts, keep)

        def sent(k, solved):
            points[steps - 1, k, place] = points[steps - 1, k, place] + (solved - late(k))

        ghosts = [late(planes + 2 * (steps - 1) + i) for i in (0, 1)]
        solve(planes, lambda k: (2.0 / wide) * late(k), lambda k: wide_ref[k], work, *ghosts, sent)
        for n in range(steps - 1):

            def old(k):
                return late(k) if n == 0 else state[k]

            def right(k):
                return (2.0 / half) * old(k)

            def keep(k, solved):
                fresh = solved - old(k)
                state[k] = fresh
                points[n, k, place] = points[n, k, place] + fresh

            ghosts = [late(planes + 2 * n + i) for i in (0, 1)]
            solve(planes, right, lambda k: fine_ref[k], work, *ghosts, keep)

    @pl.when(turn >= q_steps)
    def _():
        first = (turn - q_steps) * count
        step = 2 if count % 2 == 0 else 1
        for n in range(steps):
            lines = []
            for i in range(0, count, step):
                wide = [points[n, first + i + j].reshape(width_y, width_z) for j in range(step)]
                wide = times_left(y_ref[...], jnp.concatenate(wide, axis=1))
                lines += [wide[:, j * width_z : (j + 1) * width_z] for j in range(step)]
            block = times_right(jnp.concatenate(lines, axis=0), z_ref[...])
            out_ref[n] = block.reshape(count, width_y, width_z)


def finish(pushed, early, lates, fine_pivots, wide_pivots, y_left, z_right):
    steps, planes, parts, own, width_z = pushed.shape
    width_y = parts * own
    some = 2 if parts % 2 == 0 else 1
    count = 4 if planes % 4 == 0 else 1
    q_steps, x_steps = parts // some, planes // count
    ahead = lambda i: jnp.minimum(i, q_steps - 1)
    after = lambda i: jnp.maximum(i - q_steps, 0)
    pivots = pl.BlockSpec((planes // 2 + 1, some, own, width_z), lambda i: (0, ahead(i), 0, 0))
    return pl.pallas_call(
        lambda *refs: finish_kernel(q_steps, *refs),
        grid=(q_steps + x_steps,),
        out_shape=jax.ShapeDtypeStruct((steps, planes, width_y, width_z), jnp.float32),
        in_specs=[
            pl.BlockSpec((steps, planes, some, own, width_z), lambda i: (0, 0, ahead(i), 0, 0)),
            *(
                pl.BlockSpec((some, *late.shape[1:]), lambda i: (ahead(i), 0, 0, 0))
                for late in (early, *lates)
            ),
            pivots,
            pivots,
            pl.BlockSpec(y_left.shape, lambda i: (0, 0)),
            pl.BlockSpec(z_right.shape, lambda i: (0, 0)),
        ],
        out_specs=pl.BlockSpec((steps, count, width_y, width_z), lambda i: (0, after(i), 0, 0)),
        scratch_shapes=[
            pltpu.VMEM(pushed.shape, jnp.float32),
            pltpu.VMEM((planes, some, own, width_z), jnp.float32),
            pltpu.VMEM((planes, some, own, width_z), jnp.float32),
        ],
        cost_estimate=cost(pushed),
        compiler_params=room(60),
    )(pushed, early, *lates, fine_pivots, wide_pivots, y_left, z_right)


def per_device(forcing, coarse_guess, initial):
    steps, planes, width_y, width_z = forcing.shape
    n_space = lax.axis_size("space")
    n_plane = lax.axis_size("plane")
    width_x = planes * n_space
    parts = 2 * n_space
    own = width_y // parts
    chunks = 2 if own % 16 == 0 else 1
    rows = own // chunks
    table_x = jnp.asarray(sine_table(width_x))
    z_right = jnp.asarray(right_table(sine_table(width_z)))
    y_left = jnp.asarray(left_table(sine_table(width_y)))
    y_scaled = jnp.asarray(left_table((time_step / half) * sine_table(width_y)))
    fine_pivots = pivot_table(planes, width_y, width_z, half)
    wide_pivots = pivot_table(planes, width_y, width_z, steps * half)
    pair = lax.axis_index("pair")
    level = lax.axis_index("plane")
    offset = (lax.axis_index("space") * 2 + pair) * own
    e_x, e_y, e_z = (
        jnp.asarray(eigen_values(n).astype(np.float32)) for n in (width_x, width_y, width_z)
    )
    spectrum = (
        e_x[None, :, None]
        + lax.dynamic_slice_in_dim(e_y, offset, own)[:, None, None]
        + e_z[None, None, :]
    )
    fine = (1.0 + half * spectrum) / (1.0 - half * spectrum)
    wide = steps * half
    coarse = (1.0 + wide * spectrum) / (1.0 - wide * spectrum)
    leap = fine
    for _ in range(steps - 1):
        leap = leap * fine

    def swap(fields):
        return lax.all_to_all(fields, ("space", "pair"), split_axis=0, concat_axis=0, tiled=True)

    def spread(fields):
        return swap(fields).reshape(n_space, 2, *fields.shape[1:])

    by_device = table_x.reshape(n_space, planes, width_x)

    def modes(cells):
        return jnp.einsum("sbmqr,smp->bqpr", cells, by_device, precision=high)

    share = planes // 2
    opened = opening_fields(coarse_guess[0], initial, z_right, y_left, pair, parts)
    opened, forcing = lax.optimization_barrier((opened, forcing))
    opened = spread(opened)
    pushed, relaxed = front(
        forcing, z_right, y_scaled, jnp.asarray(fine_pivots.reshape(-1, parts, own, width_z)), parts
    )
    opened, relaxed = lax.optimization_barrier((opened, relaxed))
    arrived = spread(relaxed)

    guess = modes(opened[:, :, :planes])
    before = lax.ppermute(guess[1], "plane", [(i, (i + 1) % n_plane) for i in range(n_plane)])
    anchor = jnp.einsum(
        "sbmqr,sbmp->qpr",
        opened[:, :, planes:],
        table_x.reshape(n_space, 2, share, width_x),
        precision=high,
    )

    full = np.concatenate([np.zeros((1, width_x)), sine_table(width_x), np.zeros((1, width_x))])
    across = np.stack([full[0:width_x:planes], full[planes + 1 :: planes]], axis=1)
    across = across.astype(np.float32)
    x_left = jnp.asarray(left_table(sine_table(width_x)))
    ghost_left = jnp.asarray(ghost_table(across, steps))
    kick_left = jnp.asarray(kick_table(across, steps))
    value, second_residual, beyond = modal(
        arrived, before, guess, spectrum, (x_left, kick_left, ghost_left)
    )

    def chunk_of(array, c):
        return lax.slice_in_dim(array, c * rows, (c + 1) * rows, axis=0)

    shifted = [
        lax.ppermute(chunk_of(value[1], c), "plane", [(i, i + 1) for i in range(n_plane - 1)])
        for c in range(chunks)
    ]
    rate = [chunk_of(coarse, c) for c in range(chunks)]
    second = [chunk_of(second_residual, c) for c in range(chunks)]
    start = [chunk_of(before, c) for c in range(chunks)]
    carries = [jnp.zeros_like(start[0])] * chunks
    lasts, firsts, sent = [], [], []

    def onward(c, carried):
        return rate[c] * (rate[c] * carried + firsts[c]) + second[c]

    def hop(c, sent, place):
        return lax.ppermute(sent, "plane", [(place, place + 1)])

    swapped = []
    for c in range(chunks):
        if c > 0:
            sent[c - 1], start[c] = lax.optimization_barrier((sent[c - 1], start[c]))
        lasts.append(jnp.where(level == 0, chunk_of(anchor, c), shifted[c]))
        firsts.append(chunk_of(leap, c) * (lasts[c] - start[c]))
        sent.append(onward(c, carries[c]))
        other = jnp.where(pair == 0, second[c], firsts[c])
        swapped.append(lax.ppermute(other, "pair", [(0, 1), (1, 0)]))
    carries[0] = carries[0] + hop(0, sent[0], 0)
    following = onward(0, carries[0])
    following, lasts, swapped = lax.optimization_barrier((following, lasts, swapped))
    tables = (x_left, ghost_left)
    early = swap(to_cells(None, spectrum, tables, n_space, steps, lasts, (value, beyond)))
    for place in range(n_plane - 1):
        for c in range(chunks):
            if place > 0:
                sent[c] = following if place + c == 1 else onward(c, carries[c])
            if c < chunks - 1:
                sent[c], second[c + 1] = lax.optimization_barrier((sent[c], second[c + 1]))
            if c == chunks - 1 and place == n_plane - 2:
                sent[c], pushed = lax.optimization_barrier((sent[c], pushed))
            if place + c > 0:
                carries[c] = carries[c] + hop(c, sent[c], place)
    mine = jnp.where(pair == 0, jnp.concatenate(firsts, axis=0), second_residual)
    other = jnp.concatenate(swapped, axis=0)
    fine_pivots, wide_pivots = (
        jnp.asarray(a.reshape(-1, parts, own, width_z)) for a in (fine_pivots, wide_pivots)
    )
    early, firsts = lax.optimization_barrier((early, firsts))
    lates = []
    for c in range(chunks):
        late = to_cells(
            wide, chunk_of(spectrum, c), tables, n_space, steps, carries[c : c + 1], (firsts[c],)
        )
        late, mine = lax.optimization_barrier((late, mine))
        lates.append(swap(late))
    residual = jnp.concatenate(
        [jnp.where(pair == 0, mine, other), jnp.where(pair == 0, other, mine)], axis=0
    ).transpose(1, 0, 2)
    pushed = pushed.reshape(steps, planes, parts, own, width_z)
    points = finish(pushed, early, lates, fine_pivots, wide_pivots, y_left, z_right)
    return (points, residual[None])


def solution(mesh):
    whole = mesh.devices
    cut = Mesh(whole.reshape(whole.shape[0] // 2, 2, whole.shape[1]), ("plane", "pair", "space"))
    both = ("plane", "pair")
    placed = (P(both, "space", None, None), P(both, "space", None, None), P("space", None, None))
    return jax.shard_map(
        per_device,
        mesh=cut,
        in_specs=placed,
        out_specs=(P(both, "space", None, None), P(both, None, "space", None)),
        check_vma=False,
    )
```

```python
import jax
import jax.numpy as jnp
import ml_dtypes
import numpy as np
from jax import lax
from jax.experimental import pallas as pl
from jax.experimental.pallas import tpu as pltpu
from jax.sharding import Mesh
from jax.sharding import PartitionSpec as P

time_step = 0.5
half = 0.5 * time_step
high = lax.Precision.HIGH


def room(mebibytes):
    return pltpu.CompilerParams(vmem_limit_bytes=mebibytes << 20)


def cost(*arrays):
    moved = sum(int(np.prod(a.shape)) * 4 for a in arrays)
    return pl.CostEstimate(flops=moved * 400, bytes_accessed=2 * moved, transcendentals=0)


def sine_table(length):
    ladder = np.arange(1, length + 1, dtype=np.float64)
    table = np.sqrt(2.0 / (length + 1)) * np.sin(
        np.pi * ladder[:, None] * ladder[None, :] / (length + 1)
    )
    return table.astype(np.float32)


def eigen_values(length):
    ladder = np.arange(1, length + 1, dtype=np.float64)
    return -4.0 * np.sin(np.pi * ladder / (2 * (length + 1))) ** 2


def two_parts(table):
    upper = table.astype(ml_dtypes.bfloat16)
    return upper, (table - upper.astype(np.float32)).astype(ml_dtypes.bfloat16)


def right_table(table):
    upper, lower = two_parts(table)
    return np.block([[upper, lower], [upper, np.zeros_like(lower)]])


def left_table(table):
    upper, lower = two_parts(table)
    return np.block([[upper, upper], [lower, np.zeros_like(lower)]])


def pivot_table(planes, width_y, width_z, weight):
    cross = eigen_values(width_y)[:, None] + eigen_values(width_z)[None, :]
    diagonal = (1.0 + 2.0 * weight - weight * cross) / weight
    pivots = [1.0 / diagonal]
    for _ in range(planes // 2 - 1):
        pivots.append(1.0 / (diagonal - pivots[-1]))
    pivots.append(1.0 / (1.0 - pivots[-1] ** 2))
    return np.stack(pivots).astype(np.float32)


def ghost_table(across, steps):
    count, _, width = across.shape
    parts = two_parts(across)
    out = np.zeros((2, count, steps, 2, steps, 2, width), ml_dtypes.bfloat16)
    for n in range(steps):
        out[0, :, n, :, n, 0] = parts[0]
        out[0, :, n, :, n, 1] = parts[0]
        out[1, :, n, :, n, 0] = parts[1]
    return out.reshape(2 * count * steps * 2, steps * 2 * width)


def kick_table(across, steps):
    count, _, width = across.shape
    out = np.zeros((steps, width, 3, count, steps, 2), ml_dtypes.bfloat16)
    upper, lower = (np.transpose(a, (2, 0, 1)) for a in two_parts(across))
    for n in range(steps):
        for i, part in enumerate((upper, upper, lower)):
            out[n, :, i, :, n, :] = part
    return out.reshape(steps * width, 3 * count * steps * 2)


def split(values):
    upper = values.astype(jnp.bfloat16)
    return upper, (values - upper.astype(jnp.float32)).astype(jnp.bfloat16)


def times_right(values, table):
    width = values.shape[-1]
    both = jnp.dot(
        jnp.concatenate(split(values), axis=1), table, preferred_element_type=jnp.float32
    )
    return both[:, :width] + both[:, width:]


def times_left(table, *values):
    both = jnp.dot(
        table,
        jnp.concatenate([part for value in values for part in split(value)], axis=0),
        preferred_element_type=jnp.float32,
    )
    width = both.shape[0] // 2
    return both[:width] + both[width:]


def rates(spectrum):
    inverse = 1.0 / (1.0 - half * spectrum)
    return half * inverse, (1.0 + half * spectrum) * inverse


def side_by_side(count):
    return 2 if count % 2 == 0 else 1


def modal_kernel(
    arrived_ref, before_ref, guess_ref, spectrum_ref, x_ref, kick_ref, ghost_ref, *out_refs
):
    value_ref, second_ref, beyond_ref = out_refs
    n_space = arrived_ref.shape[0]
    own, width_x, width_z = before_ref.shape
    steps = beyond_ref.shape[2] // 2
    planes = width_x // n_space
    interval = pl.program_id(0)
    step = side_by_side(own)
    for first in range(0, own, step):
        each = range(first, first + step)

        def lines(begin, count):
            rows = [
                [arrived_ref[s, pl.ds(begin * own + q, count, stride=own), :] for q in each]
                for s in range(n_space)
            ]
            return [jnp.concatenate(row, axis=1) for row in rows]

        edges = lines(planes, 2 * steps)
        total = times_left(x_ref[...], jnp.concatenate(lines(0, planes), axis=0))
        upper, lower = split(jnp.concatenate(edges, axis=0))
        kicks = jnp.dot(
            kick_ref[...],
            jnp.concatenate([upper, lower, upper], axis=0),
            preferred_element_type=jnp.float32,
        )
        wide = lambda pieces: jnp.concatenate(list(pieces), axis=1)
        factor, fine = rates(wide(spectrum_ref[q] for q in each))
        drift, both = None, []
        for n in range(steps):
            kick = kicks[n * width_x : (n + 1) * width_x] * factor
            fresh = kick if drift is None else fine * drift + kick
            both.append(fresh if drift is None else fresh + drift)
            drift = fresh
        total = total + drift
        leap = (fine * fine) * (fine * fine) if steps == 4 else fine**steps
        guess = wide(guess_ref[q] for q in each)
        start = jnp.where(interval == 0, wide(before_ref[q] for q in each), guess)
        total = total + leap * start
        beyond = times_left(ghost_ref[...], *both)
        left = lax.broadcasted_iota(jnp.int32, edges[0].shape, 0) % 2 == 0
        blank = jnp.zeros_like(edges[0])
        for i, q in enumerate(each):
            lanes = slice(i * width_z, (i + 1) * width_z)
            value_ref[q] = total[:, lanes]
        for s in range(n_space):
            behind = pltpu.roll(edges[s - 1], 2 * steps - 1, 0) if s > 0 else blank
            ahead = pltpu.roll(edges[s + 1], 1, 0) if s < n_space - 1 else blank
            seen = beyond[s * 2 * steps : (s + 1) * 2 * steps] + jnp.where(left, behind, ahead)
            for i, q in enumerate(each):
                beyond_ref[q, s] = seen[:, i * width_z : (i + 1) * width_z]

        @pl.when(interval == 0)
        def _():
            second = leap * (total - guess)
            for i, q in enumerate(each):
                second_ref[q] = second[:, i * width_z : (i + 1) * width_z]


def modal(arrived, before, guess, spectrum, tables):
    n_space, _, total, own, width_z = arrived.shape
    width_x = before.shape[1]
    steps = (total - width_x // n_space) // 2
    still = lambda a: pl.BlockSpec(a.shape, lambda b: (0,) * a.ndim)
    lead = pl.BlockSpec((None, own, width_x, width_z), lambda b: (b, 0, 0, 0))
    return pl.pallas_call(
        modal_kernel,
        grid=(2,),
        out_shape=(
            jax.ShapeDtypeStruct((2, own, width_x, width_z), jnp.float32),
            jax.ShapeDtypeStruct((own, width_x, width_z), jnp.float32),
            jax.ShapeDtypeStruct((2, own, n_space, 2 * steps, width_z), jnp.float32),
        ),
        in_specs=[
            pl.BlockSpec((n_space, None, total * own, width_z), lambda b: (0, b, 0, 0)),
            still(before),
            pl.BlockSpec((None, own, width_x, width_z), lambda b: (0, 0, 0, 0)),
            still(spectrum),
            *(still(a) for a in tables),
        ],
        out_specs=(
            lead,
            still(before),
            pl.BlockSpec((None, own, n_space, 2 * steps, width_z), lambda b: (b, 0, 0, 0, 0)),
        ),
        cost_estimate=cost(arrived, before),
        compiler_params=room(40),
    )(arrived.reshape(n_space, 2, total * own, width_z), before, guess, spectrum, *tables)


def cells_kernel(wide_weight, lasts, spectrum_ref, x_ref, ghost_ref, *refs):
    *start_refs, out_ref = refs
    even_refs, start_refs = start_refs[:lasts], start_refs[lasts:]
    n_space = out_ref.shape[0]
    own, width_x, width_z = spectrum_ref.shape
    planes = width_x // n_space
    count = out_ref.shape[1] // own - planes
    steps = count // 2
    interval = pl.program_id(0)
    step = side_by_side(own)
    rows = own // lasts
    for first in range(0, own, step):
        each = range(first, first + step)
        wide = lambda pieces: jnp.concatenate(list(pieces), axis=1)
        spectrum = wide(spectrum_ref[q] for q in each)
        _, fine = rates(spectrum)
        even = wide(even_refs[q // rows][q % rows] for q in each)
        odd = wide(start_refs[0][q] for q in each)
        if wide_weight is not None:
            coarse = (1.0 + wide_weight * spectrum) / (1.0 - wide_weight * spectrum)
            odd = odd + coarse * even
        field = jnp.where(interval == 0, even, odd)
        both, power = [], field
        for n in range(steps if wide_weight is None else steps - 1):
            later = fine * power
            both.append(later + power)
            power = later
        if wide_weight is not None:
            both.append((coarse + 1.0) * field)
        total = times_left(x_ref[...], field)
        beyond = times_left(ghost_ref[...], *both)
        for i, q in enumerate(each):
            lanes = slice(i * width_z, (i + 1) * width_z)
            for s in range(n_space):
                seen = beyond[s * count : (s + 1) * count, lanes]
                if wide_weight is None:
                    seen = seen + start_refs[1][q, s]
                out_ref[s, pl.ds(q, planes, stride=own), :] = total[
                    s * planes : (s + 1) * planes, lanes
                ]
                out_ref[s, pl.ds(planes * own + q, count, stride=own), :] = seen


def to_cells(wide_weight, spectrum, tables, n_space, steps, evens, others):
    own, width_x, width_z = spectrum.shape
    planes = width_x // n_space
    total = planes + 2 * steps
    still = lambda a: pl.BlockSpec(a.shape, lambda b: (0,) * a.ndim)

    def placed(array):
        if array.shape[0] == 2 and array.ndim > 3:
            tail = array.shape[1:]
            pick = (lambda b: (0,) + (0,) * len(tail)) if array.ndim == 4 else (
                lambda b: (b,) + (0,) * len(tail)
            )
            return pl.BlockSpec((None, *tail), pick)
        return still(array)

    out = pl.pallas_call(
        lambda *refs: cells_kernel(wide_weight, len(evens), *refs),
        grid=(2,),
        out_shape=jax.ShapeDtypeStruct((n_space, 2, total * own, width_z), jnp.float32),
        in_specs=[
            still(spectrum),
            *(still(a) for a in tables),
            *(still(a) for a in evens),
            *(placed(a) for a in others),
        ],
        out_specs=pl.BlockSpec((n_space, None, total * own, width_z), lambda b: (0, b, 0, 0)),
        cost_estimate=cost(spectrum, spectrum),
        compiler_params=room(40),
    )(spectrum, *tables, *evens, *others)
    return out.reshape(2 * n_space, total, own, width_z)


def solve(planes, right, pivot, work, left_ghost, right_ghost, finish):
    middle = planes // 2
    lower, upper = left_ghost, right_ghost
    for k in range(middle):
        low, top = right(k), right(planes - 1 - k)
        low = low if lower is None else low + lower
        top = top if upper is None else top + upper
        factor = pivot(k)
        lower, upper = low * factor, top * factor
        if k < middle - 1:
            work[k] = lower
            work[planes - 1 - k] = upper
    factor, joint = pivot(middle - 1), pivot(middle)
    lower, upper = (lower + factor * upper) * joint, (upper + factor * lower) * joint
    finish(middle - 1, lower)
    finish(planes - middle, upper)
    for k in range(middle - 2, -1, -1):
        factor = pivot(k)
        lower = work[k] + factor * lower
        upper = work[planes - 1 - k] + factor * upper
        finish(k, lower)
        finish(planes - 1 - k, upper)


def transformed(block, z_ref, y_ref):
    count, width_y, width_z = block.shape
    lines = times_right(block.reshape(count * width_y, width_z), z_ref[...])
    step = 2 if count % 2 == 0 else 1
    out = []
    for i in range(0, count, step):
        wide = [lines[(i + j) * width_y : (i + j + 1) * width_y] for j in range(step)]
        wide = times_left(y_ref[...], jnp.concatenate(wide, axis=1))
        out += [wide[:, j * width_z : (j + 1) * width_z] for j in range(step)]
    return out


def front_kernel(x_steps, forcing_ref, z_ref, y_ref, pivot_ref, pushed_ref, out_ref, kept, work):
    steps, count, width_y, width_z = forcing_ref.shape
    planes, parts, own = kept.shape[1:4]
    some = out_ref.shape[0]
    turn = pl.program_id(0)

    @pl.when(turn < x_steps)
    def _():
        for n in range(steps):
            for i, plane in enumerate(transformed(forcing_ref[n], z_ref, y_ref)):
                pushed_ref[n, i] = plane
                kept[n, turn * count + i] = plane.reshape(parts, own, width_z)

    @pl.when(turn >= x_steps)
    def _():
        place = pl.ds((turn - x_steps) * some, some)
        for n in range(steps):

            def right(k):
                pushed = kept[n, k, place]
                return pushed if n == 0 else pushed + (2.0 / half) * out_ref[:, k]

            def finish(k, solved):
                if k == 0:
                    out_ref[:, planes + 2 * n] = solved
                if k == planes - 1:
                    out_ref[:, planes + 2 * n + 1] = solved
                out_ref[:, k] = solved if n == 0 else solved - out_ref[:, k]

            solve(planes, right, lambda k: pivot_ref[k], work, None, None, finish)


def front(forcing, z_right, y_left, pivots, parts):
    steps, planes, width_y, width_z = forcing.shape
    own = width_y // parts
    count = 4 if planes % 4 == 0 else 1
    some = 2 if parts % 2 == 0 else 1
    x_steps, q_steps = planes // count, parts // some
    early = lambda i: jnp.minimum(i, x_steps - 1)
    late = lambda i: jnp.maximum(i - x_steps, 0)
    total = planes + 2 * steps
    return pl.pallas_call(
        lambda *refs: front_kernel(x_steps, *refs),
        grid=(x_steps + q_steps,),
        out_shape=(
            jax.ShapeDtypeStruct(forcing.shape, jnp.float32),
            jax.ShapeDtypeStruct((parts, total, own, width_z), jnp.float32),
        ),
        in_specs=[
            pl.BlockSpec((steps, count, width_y, width_z), lambda i: (0, early(i), 0, 0)),
            pl.BlockSpec(z_right.shape, lambda i: (0, 0)),
            pl.BlockSpec(y_left.shape, lambda i: (0, 0)),
            pl.BlockSpec((planes // 2 + 1, some, own, width_z), lambda i: (0, late(i), 0, 0)),
        ],
        out_specs=(
            pl.BlockSpec((steps, count, width_y, width_z), lambda i: (0, early(i), 0, 0)),
            pl.BlockSpec((some, total, own, width_z), lambda i: (late(i), 0, 0, 0)),
        ),
        scratch_shapes=[
            pltpu.VMEM((steps, planes, parts, own, width_z), jnp.float32),
            pltpu.VMEM((planes, some, own, width_z), jnp.float32),
        ],
        cost_estimate=cost(forcing),
        compiler_params=room(24),
    )(forcing, z_right, y_left, pivots)


def opening_kernel(g_steps, pair_ref, guess_ref, initial_ref, z_ref, y_ref, out_ref):
    parts, count, own, width_z = out_ref.shape
    block = jnp.where(pl.program_id(0) < g_steps, guess_ref[...], initial_ref[...])
    for i, plane in enumerate(transformed(block, z_ref, y_ref)):
        out_ref[:, i] = plane.reshape(parts, own, width_z)


def opening_fields(guess, initial, z_right, y_left, pair, parts):
    planes, width_y, width_z = guess.shape
    share = planes // 2
    count = next(c for c in (16, 8, 1) if share % c == 0)
    g_steps, a_steps = planes // count, share // count
    own = width_y // parts
    block = (count, width_y, width_z)
    whole = lambda a: pl.BlockSpec(a.shape, lambda i, p: (0, 0))
    return pl.pallas_call(
        lambda *refs: opening_kernel(g_steps, *refs),
        grid_spec=pltpu.PrefetchScalarGridSpec(
            num_scalar_prefetch=1,
            grid=(g_steps + a_steps,),
            in_specs=[
                pl.BlockSpec(block, lambda i, p: (jnp.minimum(i, g_steps - 1), 0, 0)),
                pl.BlockSpec(
                    block, lambda i, p: (p[0] * a_steps + jnp.maximum(i - g_steps, 0), 0, 0)
                ),
                whole(z_right),
                whole(y_left),
            ],
            out_specs=pl.BlockSpec((parts, count, own, width_z), lambda i, p: (0, i, 0, 0)),
        ),
        out_shape=jax.ShapeDtypeStruct((parts, planes + share, own, width_z), jnp.float32),
        cost_estimate=cost(guess),
        compiler_params=room(60),
    )(pair[None], guess, initial, z_right, y_left)


def finish_kernel(q_steps, pushed_ref, early_ref, *refs):
    *late_refs, fine_ref, wide_ref, y_ref, z_ref, out_ref, points, state, work = refs
    steps, count, width_y, width_z = out_ref.shape
    planes = points.shape[1]
    some = state.shape[1]
    wide = steps * half
    turn = pl.program_id(0)

    def late(k):
        return jnp.concatenate([ref[:, k] for ref in late_refs], axis=1)

    @pl.when(turn < q_steps)
    def _():
        place = pl.ds(turn * some, some)
        for n in range(steps):

            def old(k):
                return early_ref[:, k] if n == 0 else points[n - 1, k, place]

            def right(k):
                return pushed_ref[n, k] + (2.0 / half) * old(k)

            def keep(k, solved):
                points[n, k, place] = solved - old(k)

            ghosts = [early_ref[:, planes + 2 * n + i] for i in (0, 1)]
            solve(planes, right, lambda k: fine_ref[k], work, *ghosts, keep)

        def sent(k, solved):
            points[steps - 1, k, place] = points[steps - 1, k, place] + (solved - late(k))

        ghosts = [late(planes + 2 * (steps - 1) + i) for i in (0, 1)]
        solve(planes, lambda k: (2.0 / wide) * late(k), lambda k: wide_ref[k], work, *ghosts, sent)
        for n in range(steps - 1):

            def old(k):
                return late(k) if n == 0 else state[k]

            def right(k):
                return (2.0 / half) * old(k)

            def keep(k, solved):
                fresh = solved - old(k)
                state[k] = fresh
                points[n, k, place] = points[n, k, place] + fresh

            ghosts = [late(planes + 2 * n + i) for i in (0, 1)]
            solve(planes, right, lambda k: fine_ref[k], work, *ghosts, keep)

    @pl.when(turn >= q_steps)
    def _():
        first = (turn - q_steps) * count
        step = 2 if count % 2 == 0 else 1
        for n in range(steps):
            lines = []
            for i in range(0, count, step):
                wide = [points[n, first + i + j].reshape(width_y, width_z) for j in range(step)]
                wide = times_left(y_ref[...], jnp.concatenate(wide, axis=1))
                lines += [wide[:, j * width_z : (j + 1) * width_z] for j in range(step)]
            block = times_right(jnp.concatenate(lines, axis=0), z_ref[...])
            out_ref[n] = block.reshape(count, width_y, width_z)


def finish(pushed, early, lates, fine_pivots, wide_pivots, y_left, z_right):
    steps, planes, parts, own, width_z = pushed.shape
    width_y = parts * own
    some = next(c for c in (4, 2, 1) if parts % c == 0)
    count = next(c for c in (8, 4, 1) if planes % c == 0)
    q_steps, x_steps = parts // some, planes // count
    ahead = lambda i: jnp.minimum(i, q_steps - 1)
    after = lambda i: jnp.maximum(i - q_steps, 0)
    pivots = pl.BlockSpec((planes // 2 + 1, some, own, width_z), lambda i: (0, ahead(i), 0, 0))
    return pl.pallas_call(
        lambda *refs: finish_kernel(q_steps, *refs),
        grid=(q_steps + x_steps,),
        out_shape=jax.ShapeDtypeStruct((steps, planes, width_y, width_z), jnp.float32),
        in_specs=[
            pl.BlockSpec((steps, planes, some, own, width_z), lambda i: (0, 0, ahead(i), 0, 0)),
            *(
                pl.BlockSpec((some, *late.shape[1:]), lambda i: (ahead(i), 0, 0, 0))
                for late in (early, *lates)
            ),
            pivots,
            pivots,
            pl.BlockSpec(y_left.shape, lambda i: (0, 0)),
            pl.BlockSpec(z_right.shape, lambda i: (0, 0)),
        ],
        out_specs=pl.BlockSpec((steps, count, width_y, width_z), lambda i: (0, after(i), 0, 0)),
        scratch_shapes=[
            pltpu.VMEM(pushed.shape, jnp.float32),
            pltpu.VMEM((planes, some, own, width_z), jnp.float32),
            pltpu.VMEM((planes, some, own, width_z), jnp.float32),
        ],
        cost_estimate=cost(pushed),
        compiler_params=room(60),
    )(pushed, early, *lates, fine_pivots, wide_pivots, y_left, z_right)


def per_device(forcing, coarse_guess, initial):
    steps, planes, width_y, width_z = forcing.shape
    n_space = lax.axis_size("space")
    n_plane = lax.axis_size("plane")
    width_x = planes * n_space
    parts = 2 * n_space
    own = width_y // parts
    chunks = 2 if own % 16 == 0 else 1
    rows = own // chunks
    table_x = jnp.asarray(sine_table(width_x))
    z_right = jnp.asarray(right_table(sine_table(width_z)))
    y_left = jnp.asarray(left_table(sine_table(width_y)))
    y_scaled = jnp.asarray(left_table((time_step / half) * sine_table(width_y)))
    fine_pivots = pivot_table(planes, width_y, width_z, half)
    wide_pivots = pivot_table(planes, width_y, width_z, steps * half)
    pair = lax.axis_index("pair")
    level = lax.axis_index("plane")
    offset = (lax.axis_index("space") * 2 + pair) * own
    e_x, e_y, e_z = (
        jnp.asarray(eigen_values(n).astype(np.float32)) for n in (width_x, width_y, width_z)
    )
    spectrum = (
        e_x[None, :, None]
        + lax.dynamic_slice_in_dim(e_y, offset, own)[:, None, None]
        + e_z[None, None, :]
    )
    fine = (1.0 + half * spectrum) / (1.0 - half * spectrum)
    wide = steps * half
    coarse = (1.0 + wide * spectrum) / (1.0 - wide * spectrum)
    leap = fine
    for _ in range(steps - 1):
        leap = leap * fine

    def swap(fields):
        return lax.all_to_all(fields, ("space", "pair"), split_axis=0, concat_axis=0, tiled=True)

    def spread(fields):
        return swap(fields).reshape(n_space, 2, *fields.shape[1:])

    by_device = table_x.reshape(n_space, planes, width_x)

    def modes(cells):
        return jnp.einsum("sbmqr,smp->bqpr", cells, by_device, precision=high)

    share = planes // 2
    opened = opening_fields(coarse_guess[0], initial, z_right, y_left, pair, parts)
    opened, forcing = lax.optimization_barrier((opened, forcing))
    opened = spread(opened)
    pushed, relaxed = front(
        forcing, z_right, y_scaled, jnp.asarray(fine_pivots.reshape(-1, parts, own, width_z)), parts
    )
    opened, relaxed = lax.optimization_barrier((opened, relaxed))
    arrived = spread(relaxed)

    guess = modes(opened[:, :, :planes])
    before = lax.ppermute(guess[1], "plane", [(i, (i + 1) % n_plane) for i in range(n_plane)])
    anchor = jnp.einsum(
        "sbmqr,sbmp->qpr",
        opened[:, :, planes:],
        table_x.reshape(n_space, 2, share, width_x),
        precision=high,
    )

    full = np.concatenate([np.zeros((1, width_x)), sine_table(width_x), np.zeros((1, width_x))])
    across = np.stack([full[0:width_x:planes], full[planes + 1 :: planes]], axis=1)
    across = across.astype(np.float32)
    x_left = jnp.asarray(left_table(sine_table(width_x)))
    ghost_left = jnp.asarray(ghost_table(across, steps))
    kick_left = jnp.asarray(kick_table(across, steps))
    value, second_residual, beyond = modal(
        arrived, before, guess, spectrum, (x_left, kick_left, ghost_left)
    )

    def chunk_of(array, c):
        return lax.slice_in_dim(array, c * rows, (c + 1) * rows, axis=0)

    shifted = [
        lax.ppermute(chunk_of(value[1], c), "plane", [(i, i + 1) for i in range(n_plane - 1)])
        for c in range(chunks)
    ]
    rate = [chunk_of(coarse, c) for c in range(chunks)]
    second = [chunk_of(second_residual, c) for c in range(chunks)]
    start = [chunk_of(before, c) for c in range(chunks)]
    carries = [jnp.zeros_like(start[0])] * chunks
    lasts, firsts, sent = [], [], []

    def onward(c, carried):
        return rate[c] * (rate[c] * carried + firsts[c]) + second[c]

    def hop(c, sent, place):
        return lax.ppermute(sent, "plane", [(place, place + 1)])

    swapped = []
    for c in range(chunks):
        if c > 0:
            sent[c - 1], start[c] = lax.optimization_barrier((sent[c - 1], start[c]))
        lasts.append(jnp.where(level == 0, chunk_of(anchor, c), shifted[c]))
        firsts.append(chunk_of(leap, c) * (lasts[c] - start[c]))
        sent.append(onward(c, carries[c]))
        other = jnp.where(pair == 0, second[c], firsts[c])
        swapped.append(lax.ppermute(other, "pair", [(0, 1), (1, 0)]))
    carries[0] = carries[0] + hop(0, sent[0], 0)
    following = onward(0, carries[0])
    following, lasts, swapped = lax.optimization_barrier((following, lasts, swapped))
    tables = (x_left, ghost_left)
    early = swap(to_cells(None, spectrum, tables, n_space, steps, lasts, (value, beyond)))
    for place in range(n_plane - 1):
        for c in range(chunks):
            if place > 0:
                sent[c] = following if place + c == 1 else onward(c, carries[c])
            if c < chunks - 1:
                sent[c], second[c + 1] = lax.optimization_barrier((sent[c], second[c + 1]))
            if c == chunks - 1 and place == n_plane - 2:
                sent[c], pushed = lax.optimization_barrier((sent[c], pushed))
            if place + c > 0:
                carries[c] = carries[c] + hop(c, sent[c], place)
    mine = jnp.where(pair == 0, jnp.concatenate(firsts, axis=0), second_residual)
    other = jnp.concatenate(swapped, axis=0)
    fine_pivots, wide_pivots = (
        jnp.asarray(a.reshape(-1, parts, own, width_z)) for a in (fine_pivots, wide_pivots)
    )
    early, firsts = lax.optimization_barrier((early, firsts))
    lates = []
    for c in range(chunks):
        late = to_cells(
            wide, chunk_of(spectrum, c), tables, n_space, steps, carries[c : c + 1], (firsts[c],)
        )
        late, mine = lax.optimization_barrier((late, mine))
        lates.append(swap(late))
    residual = jnp.concatenate(
        [jnp.where(pair == 0, mine, other), jnp.where(pair == 0, other, mine)], axis=0
    ).transpose(1, 0, 2)
    pushed = pushed.reshape(steps, planes, parts, own, width_z)
    points = finish(pushed, early, lates, fine_pivots, wide_pivots, y_left, z_right)
    return (points, residual[None])


def solution(mesh):
    whole = mesh.devices
    cut = Mesh(whole.reshape(whole.shape[0] // 2, 2, whole.shape[1]), ("plane", "pair", "space"))
    both = ("plane", "pair")
    placed = (P(both, "space", None, None), P(both, "space", None, None), P("space", None, None))
    return jax.shard_map(
        per_device,
        mesh=cut,
        in_specs=placed,
        out_specs=(P(both, "space", None, None), P(both, None, "space", None)),
        check_vma=False,
    )
```

```python
import jax
import jax.numpy as jnp
import ml_dtypes
import numpy as np
from jax import lax
from jax.experimental import pallas as pl
from jax.experimental.pallas import tpu as pltpu
from jax.sharding import Mesh
from jax.sharding import PartitionSpec as P

time_step = 0.5
half = 0.5 * time_step
high = lax.Precision.HIGH


def room(mebibytes):
    return pltpu.CompilerParams(vmem_limit_bytes=mebibytes << 20)


def cost(*arrays):
    moved = sum(int(np.prod(a.shape)) * 4 for a in arrays)
    return pl.CostEstimate(flops=moved * 400, bytes_accessed=2 * moved, transcendentals=0)


def sine_table(length):
    ladder = np.arange(1, length + 1, dtype=np.float64)
    table = np.sqrt(2.0 / (length + 1)) * np.sin(
        np.pi * ladder[:, None] * ladder[None, :] / (length + 1)
    )
    return table.astype(np.float32)


def eigen_values(length):
    ladder = np.arange(1, length + 1, dtype=np.float64)
    return -4.0 * np.sin(np.pi * ladder / (2 * (length + 1))) ** 2


def two_parts(table):
    upper = table.astype(ml_dtypes.bfloat16)
    return upper, (table - upper.astype(np.float32)).astype(ml_dtypes.bfloat16)


def right_table(table):
    upper, lower = two_parts(table)
    return np.block([[upper, lower], [upper, np.zeros_like(lower)]])


def left_table(table):
    upper, lower = two_parts(table)
    return np.block([[upper, upper], [lower, np.zeros_like(lower)]])


def pivot_table(planes, width_y, width_z, weight):
    cross = eigen_values(width_y)[:, None] + eigen_values(width_z)[None, :]
    diagonal = (1.0 + 2.0 * weight - weight * cross) / weight
    pivots = [1.0 / diagonal]
    for _ in range(planes // 2 - 1):
        pivots.append(1.0 / (diagonal - pivots[-1]))
    pivots.append(1.0 / (1.0 - pivots[-1] ** 2))
    return np.stack(pivots).astype(np.float32)


def ghost_table(across, steps):
    count, _, width = across.shape
    parts = two_parts(across)
    out = np.zeros((2, count, steps, 2, steps, 2, width), ml_dtypes.bfloat16)
    for n in range(steps):
        out[0, :, n, :, n, 0] = parts[0]
        out[0, :, n, :, n, 1] = parts[0]
        out[1, :, n, :, n, 0] = parts[1]
    return out.reshape(2 * count * steps * 2, steps * 2 * width)


def kick_table(across, steps):
    count, _, width = across.shape
    out = np.zeros((steps, width, 3, count, steps, 2), ml_dtypes.bfloat16)
    upper, lower = (np.transpose(a, (2, 0, 1)) for a in two_parts(across))
    for n in range(steps):
        for i, part in enumerate((upper, upper, lower)):
            out[n, :, i, :, n, :] = part
    return out.reshape(steps * width, 3 * count * steps * 2)


def split(values):
    upper = values.astype(jnp.bfloat16)
    return upper, (values - upper.astype(jnp.float32)).astype(jnp.bfloat16)


def times_right(values, table):
    width = values.shape[-1]
    both = jnp.dot(
        jnp.concatenate(split(values), axis=1), table, preferred_element_type=jnp.float32
    )
    return both[:, :width] + both[:, width:]


def times_left(table, *values):
    both = jnp.dot(
        table,
        jnp.concatenate([part for value in values for part in split(value)], axis=0),
        preferred_element_type=jnp.float32,
    )
    width = both.shape[0] // 2
    return both[:width] + both[width:]


def rates(spectrum):
    inverse = 1.0 / (1.0 - half * spectrum)
    return half * inverse, (1.0 + half * spectrum) * inverse


def side_by_side(count):
    return 2 if count % 2 == 0 else 1


def modal_kernel(
    arrived_ref, before_ref, guess_ref, spectrum_ref, x_ref, kick_ref, ghost_ref, *out_refs
):
    value_ref, second_ref, beyond_ref = out_refs
    n_space = arrived_ref.shape[0]
    own, width_x, width_z = before_ref.shape
    steps = beyond_ref.shape[2] // 2
    planes = width_x // n_space
    interval = pl.program_id(0)
    step = side_by_side(own)
    for first in range(0, own, step):
        each = range(first, first + step)

        def lines(begin, count):
            rows = [
                [arrived_ref[s, pl.ds(begin * own + q, count, stride=own), :] for q in each]
                for s in range(n_space)
            ]
            return [jnp.concatenate(row, axis=1) for row in rows]

        edges = lines(planes, 2 * steps)
        total = times_left(x_ref[...], jnp.concatenate(lines(0, planes), axis=0))
        upper, lower = split(jnp.concatenate(edges, axis=0))
        kicks = jnp.dot(
            kick_ref[...],
            jnp.concatenate([upper, lower, upper], axis=0),
            preferred_element_type=jnp.float32,
        )
        wide = lambda pieces: jnp.concatenate(list(pieces), axis=1)
        factor, fine = rates(wide(spectrum_ref[q] for q in each))
        drift, both = None, []
        for n in range(steps):
            kick = kicks[n * width_x : (n + 1) * width_x] * factor
            fresh = kick if drift is None else fine * drift + kick
            both.append(fresh if drift is None else fresh + drift)
            drift = fresh
        total = total + drift
        leap = (fine * fine) * (fine * fine) if steps == 4 else fine**steps
        guess = wide(guess_ref[q] for q in each)
        start = jnp.where(interval == 0, wide(before_ref[q] for q in each), guess)
        total = total + leap * start
        beyond = times_left(ghost_ref[...], *both)
        left = lax.broadcasted_iota(jnp.int32, edges[0].shape, 0) % 2 == 0
        blank = jnp.zeros_like(edges[0])
        for i, q in enumerate(each):
            lanes = slice(i * width_z, (i + 1) * width_z)
            value_ref[q] = total[:, lanes]
        for s in range(n_space):
            behind = pltpu.roll(edges[s - 1], 2 * steps - 1, 0) if s > 0 else blank
            ahead = pltpu.roll(edges[s + 1], 1, 0) if s < n_space - 1 else blank
            seen = beyond[s * 2 * steps : (s + 1) * 2 * steps] + jnp.where(left, behind, ahead)
            for i, q in enumerate(each):
                beyond_ref[q, s] = seen[:, i * width_z : (i + 1) * width_z]

        @pl.when(interval == 0)
        def _():
            second = leap * (total - guess)
            for i, q in enumerate(each):
                second_ref[q] = second[:, i * width_z : (i + 1) * width_z]


def modal(arrived, before, guess, spectrum, tables):
    n_space, _, total, own, width_z = arrived.shape
    width_x = before.shape[1]
    steps = (total - width_x // n_space) // 2
    still = lambda a: pl.BlockSpec(a.shape, lambda b: (0,) * a.ndim)
    lead = pl.BlockSpec((None, own, width_x, width_z), lambda b: (b, 0, 0, 0))
    return pl.pallas_call(
        modal_kernel,
        grid=(2,),
        out_shape=(
            jax.ShapeDtypeStruct((2, own, width_x, width_z), jnp.float32),
            jax.ShapeDtypeStruct((own, width_x, width_z), jnp.float32),
            jax.ShapeDtypeStruct((2, own, n_space, 2 * steps, width_z), jnp.float32),
        ),
        in_specs=[
            pl.BlockSpec((n_space, None, total * own, width_z), lambda b: (0, b, 0, 0)),
            still(before),
            pl.BlockSpec((None, own, width_x, width_z), lambda b: (0, 0, 0, 0)),
            still(spectrum),
            *(still(a) for a in tables),
        ],
        out_specs=(
            lead,
            still(before),
            pl.BlockSpec((None, own, n_space, 2 * steps, width_z), lambda b: (b, 0, 0, 0, 0)),
        ),
        cost_estimate=cost(arrived, before),
        compiler_params=room(60),
    )(arrived.reshape(n_space, 2, total * own, width_z), before, guess, spectrum, *tables)


def cells_kernel(wide_weight, lasts, spectrum_ref, x_ref, ghost_ref, *refs):
    *start_refs, out_ref = refs
    even_refs, start_refs = start_refs[:lasts], start_refs[lasts:]
    n_space = out_ref.shape[0]
    own, width_x, width_z = spectrum_ref.shape
    planes = width_x // n_space
    count = out_ref.shape[1] // own - planes
    steps = count // 2
    interval = pl.program_id(0)
    step = side_by_side(own)
    rows = own // lasts
    for first in range(0, own, step):
        each = range(first, first + step)
        wide = lambda pieces: jnp.concatenate(list(pieces), axis=1)
        spectrum = wide(spectrum_ref[q] for q in each)
        _, fine = rates(spectrum)
        even = wide(even_refs[q // rows][q % rows] for q in each)
        odd = wide(start_refs[0][q] for q in each)
        if wide_weight is not None:
            coarse = (1.0 + wide_weight * spectrum) / (1.0 - wide_weight * spectrum)
            odd = odd + coarse * even
        field = jnp.where(interval == 0, even, odd)
        both, power = [], field
        for n in range(steps if wide_weight is None else steps - 1):
            later = fine * power
            both.append(later + power)
            power = later
        if wide_weight is not None:
            both.append((coarse + 1.0) * field)
        total = times_left(x_ref[...], field)
        beyond = times_left(ghost_ref[...], *both)
        for i, q in enumerate(each):
            lanes = slice(i * width_z, (i + 1) * width_z)
            for s in range(n_space):
                seen = beyond[s * count : (s + 1) * count, lanes]
                if wide_weight is None:
                    seen = seen + start_refs[1][q, s]
                out_ref[s, pl.ds(q, planes, stride=own), :] = total[
                    s * planes : (s + 1) * planes, lanes
                ]
                out_ref[s, pl.ds(planes * own + q, count, stride=own), :] = seen


def to_cells(wide_weight, spectrum, tables, n_space, steps, evens, others):
    own, width_x, width_z = spectrum.shape
    planes = width_x // n_space
    total = planes + 2 * steps
    still = lambda a: pl.BlockSpec(a.shape, lambda b: (0,) * a.ndim)

    def placed(array):
        if array.shape[0] == 2 and array.ndim > 3:
            tail = array.shape[1:]
            pick = (lambda b: (0,) + (0,) * len(tail)) if array.ndim == 4 else (
                lambda b: (b,) + (0,) * len(tail)
            )
            return pl.BlockSpec((None, *tail), pick)
        return still(array)

    out = pl.pallas_call(
        lambda *refs: cells_kernel(wide_weight, len(evens), *refs),
        grid=(2,),
        out_shape=jax.ShapeDtypeStruct((n_space, 2, total * own, width_z), jnp.float32),
        in_specs=[
            still(spectrum),
            *(still(a) for a in tables),
            *(still(a) for a in evens),
            *(placed(a) for a in others),
        ],
        out_specs=pl.BlockSpec((n_space, None, total * own, width_z), lambda b: (0, b, 0, 0)),
        cost_estimate=cost(spectrum, spectrum),
        compiler_params=room(60),
    )(spectrum, *tables, *evens, *others)
    return out.reshape(2 * n_space, total, own, width_z)


def solve(planes, right, pivot, work, left_ghost, right_ghost, finish):
    middle = planes // 2
    lower, upper = left_ghost, right_ghost
    for k in range(middle):
        low, top = right(k), right(planes - 1 - k)
        low = low if lower is None else low + lower
        top = top if upper is None else top + upper
        factor = pivot(k)
        lower, upper = low * factor, top * factor
        if k < middle - 1:
            work[k] = lower
            work[planes - 1 - k] = upper
    factor, joint = pivot(middle - 1), pivot(middle)
    lower, upper = (lower + factor * upper) * joint, (upper + factor * lower) * joint
    finish(middle - 1, lower)
    finish(planes - middle, upper)
    for k in range(middle - 2, -1, -1):
        factor = pivot(k)
        lower = work[k] + factor * lower
        upper = work[planes - 1 - k] + factor * upper
        finish(k, lower)
        finish(planes - 1 - k, upper)


def transformed(block, z_ref, y_ref):
    count, width_y, width_z = block.shape
    lines = times_right(block.reshape(count * width_y, width_z), z_ref[...])
    step = 2 if count % 2 == 0 else 1
    out = []
    for i in range(0, count, step):
        wide = [lines[(i + j) * width_y : (i + j + 1) * width_y] for j in range(step)]
        wide = times_left(y_ref[...], jnp.concatenate(wide, axis=1))
        out += [wide[:, j * width_z : (j + 1) * width_z] for j in range(step)]
    return out


def front_kernel(x_steps, forcing_ref, z_ref, y_ref, pivot_ref, pushed_ref, out_ref, kept, work):
    steps, count, width_y, width_z = forcing_ref.shape
    planes, parts, own = kept.shape[1:4]
    some = out_ref.shape[0]
    turn = pl.program_id(0)

    @pl.when(turn < x_steps)
    def _():
        for n in range(steps):
            for i, plane in enumerate(transformed(forcing_ref[n], z_ref, y_ref)):
                pushed_ref[n, i] = plane
                kept[n, turn * count + i] = plane.reshape(parts, own, width_z)

    @pl.when(turn >= x_steps)
    def _():
        place = pl.ds((turn - x_steps) * some, some)
        for n in range(steps):

            def right(k):
                pushed = kept[n, k, place]
                return pushed if n == 0 else pushed + (2.0 / half) * out_ref[:, k]

            def finish(k, solved):
                if k == 0:
                    out_ref[:, planes + 2 * n] = solved
                if k == planes - 1:
                    out_ref[:, planes + 2 * n + 1] = solved
                out_ref[:, k] = solved if n == 0 else solved - out_ref[:, k]

            solve(planes, right, lambda k: pivot_ref[k], work, None, None, finish)


def front(forcing, z_right, y_left, pivots, parts):
    steps, planes, width_y, width_z = forcing.shape
    own = width_y // parts
    count = 4 if planes % 4 == 0 else 1
    some = 2 if parts % 2 == 0 else 1
    x_steps, q_steps = planes // count, parts // some
    early = lambda i: jnp.minimum(i, x_steps - 1)
    late = lambda i: jnp.maximum(i - x_steps, 0)
    total = planes + 2 * steps
    return pl.pallas_call(
        lambda *refs: front_kernel(x_steps, *refs),
        grid=(x_steps + q_steps,),
        out_shape=(
            jax.ShapeDtypeStruct(forcing.shape, jnp.float32),
            jax.ShapeDtypeStruct((parts, total, own, width_z), jnp.float32),
        ),
        in_specs=[
            pl.BlockSpec((steps, count, width_y, width_z), lambda i: (0, early(i), 0, 0)),
            pl.BlockSpec(z_right.shape, lambda i: (0, 0)),
            pl.BlockSpec(y_left.shape, lambda i: (0, 0)),
            pl.BlockSpec((planes // 2 + 1, some, own, width_z), lambda i: (0, late(i), 0, 0)),
        ],
        out_specs=(
            pl.BlockSpec((steps, count, width_y, width_z), lambda i: (0, early(i), 0, 0)),
            pl.BlockSpec((some, total, own, width_z), lambda i: (late(i), 0, 0, 0)),
        ),
        scratch_shapes=[
            pltpu.VMEM((steps, planes, parts, own, width_z), jnp.float32),
            pltpu.VMEM((planes, some, own, width_z), jnp.float32),
        ],
        cost_estimate=cost(forcing),
        compiler_params=room(24),
    )(forcing, z_right, y_left, pivots)


def opening_kernel(g_steps, pair_ref, guess_ref, initial_ref, z_ref, y_ref, out_ref):
    parts, count, own, width_z = out_ref.shape
    block = jnp.where(pl.program_id(0) < g_steps, guess_ref[...], initial_ref[...])
    for i, plane in enumerate(transformed(block, z_ref, y_ref)):
        out_ref[:, i] = plane.reshape(parts, own, width_z)


def opening_fields(guess, initial, z_right, y_left, pair, parts):
    planes, width_y, width_z = guess.shape
    share = planes // 2
    count = next(c for c in (16, 8, 1) if share % c == 0)
    g_steps, a_steps = planes // count, share // count
    own = width_y // parts
    block = (count, width_y, width_z)
    whole = lambda a: pl.BlockSpec(a.shape, lambda i, p: (0, 0))
    return pl.pallas_call(
        lambda *refs: opening_kernel(g_steps, *refs),
        grid_spec=pltpu.PrefetchScalarGridSpec(
            num_scalar_prefetch=1,
            grid=(g_steps + a_steps,),
            in_specs=[
                pl.BlockSpec(block, lambda i, p: (jnp.minimum(i, g_steps - 1), 0, 0)),
                pl.BlockSpec(
                    block, lambda i, p: (p[0] * a_steps + jnp.maximum(i - g_steps, 0), 0, 0)
                ),
                whole(z_right),
                whole(y_left),
            ],
            out_specs=pl.BlockSpec((parts, count, own, width_z), lambda i, p: (0, i, 0, 0)),
        ),
        out_shape=jax.ShapeDtypeStruct((parts, planes + share, own, width_z), jnp.float32),
        cost_estimate=cost(guess),
        compiler_params=room(60),
    )(pair[None], guess, initial, z_right, y_left)


def finish_kernel(q_steps, pushed_ref, early_ref, *refs):
    *late_refs, fine_ref, wide_ref, y_ref, z_ref, out_ref, points, state, work = refs
    steps, count, width_y, width_z = out_ref.shape
    planes = points.shape[1]
    some = state.shape[1]
    wide = steps * half
    turn = pl.program_id(0)

    def late(k):
        return jnp.concatenate([ref[:, k] for ref in late_refs], axis=1)

    @pl.when(turn < q_steps)
    def _():
        place = pl.ds(turn * some, some)
        for n in range(steps):

            def old(k):
                return early_ref[:, k] if n == 0 else points[n - 1, k, place]

            def right(k):
                return pushed_ref[n, k] + (2.0 / half) * old(k)

            def keep(k, solved):
                points[n, k, place] = solved - old(k)

            ghosts = [early_ref[:, planes + 2 * n + i] for i in (0, 1)]
            solve(planes, right, lambda k: fine_ref[k], work, *ghosts, keep)

        def sent(k, solved):
            points[steps - 1, k, place] = points[steps - 1, k, place] + (solved - late(k))

        ghosts = [late(planes + 2 * (steps - 1) + i) for i in (0, 1)]
        solve(planes, lambda k: (2.0 / wide) * late(k), lambda k: wide_ref[k], work, *ghosts, sent)
        for n in range(steps - 1):

            def old(k):
                return late(k) if n == 0 else state[k]

            def right(k):
                return (2.0 / half) * old(k)

            def keep(k, solved):
                fresh = solved - old(k)
                state[k] = fresh
                points[n, k, place] = points[n, k, place] + fresh

            ghosts = [late(planes + 2 * n + i) for i in (0, 1)]
            solve(planes, right, lambda k: fine_ref[k], work, *ghosts, keep)

    @pl.when(turn >= q_steps)
    def _():
        first = (turn - q_steps) * count
        step = 2 if count % 2 == 0 else 1
        for n in range(steps):
            lines = []
            for i in range(0, count, step):
                wide = [points[n, first + i + j].reshape(width_y, width_z) for j in range(step)]
                wide = times_left(y_ref[...], jnp.concatenate(wide, axis=1))
                lines += [wide[:, j * width_z : (j + 1) * width_z] for j in range(step)]
            block = times_right(jnp.concatenate(lines, axis=0), z_ref[...])
            out_ref[n] = block.reshape(count, width_y, width_z)


def finish(pushed, early, lates, fine_pivots, wide_pivots, y_left, z_right):
    steps, planes, parts, own, width_z = pushed.shape
    width_y = parts * own
    some = next(c for c in (4, 2, 1) if parts % c == 0)
    count = next(c for c in (8, 4, 1) if planes % c == 0)
    q_steps, x_steps = parts // some, planes // count
    ahead = lambda i: jnp.minimum(i, q_steps - 1)
    after = lambda i: jnp.maximum(i - q_steps, 0)
    pivots = pl.BlockSpec((planes // 2 + 1, some, own, width_z), lambda i: (0, ahead(i), 0, 0))
    return pl.pallas_call(
        lambda *refs: finish_kernel(q_steps, *refs),
        grid=(q_steps + x_steps,),
        out_shape=jax.ShapeDtypeStruct((steps, planes, width_y, width_z), jnp.float32),
        in_specs=[
            pl.BlockSpec((steps, planes, some, own, width_z), lambda i: (0, 0, ahead(i), 0, 0)),
            *(
                pl.BlockSpec((some, *late.shape[1:]), lambda i: (ahead(i), 0, 0, 0))
                for late in (early, *lates)
            ),
            pivots,
            pivots,
            pl.BlockSpec(y_left.shape, lambda i: (0, 0)),
            pl.BlockSpec(z_right.shape, lambda i: (0, 0)),
        ],
        out_specs=pl.BlockSpec((steps, count, width_y, width_z), lambda i: (0, after(i), 0, 0)),
        scratch_shapes=[
            pltpu.VMEM(pushed.shape, jnp.float32),
            pltpu.VMEM((planes, some, own, width_z), jnp.float32),
            pltpu.VMEM((planes, some, own, width_z), jnp.float32),
        ],
        cost_estimate=cost(pushed),
        compiler_params=room(60),
    )(pushed, early, *lates, fine_pivots, wide_pivots, y_left, z_right)


def per_device(forcing, coarse_guess, initial):
    steps, planes, width_y, width_z = forcing.shape
    n_space = lax.axis_size("space")
    n_plane = lax.axis_size("plane")
    width_x = planes * n_space
    parts = 2 * n_space
    own = width_y // parts
    chunks = 2 if own % 16 == 0 else 1
    rows = own // chunks
    table_x = jnp.asarray(sine_table(width_x))
    z_right = jnp.asarray(right_table(sine_table(width_z)))
    y_left = jnp.asarray(left_table(sine_table(width_y)))
    y_scaled = jnp.asarray(left_table((time_step / half) * sine_table(width_y)))
    fine_pivots = pivot_table(planes, width_y, width_z, half)
    wide_pivots = pivot_table(planes, width_y, width_z, steps * half)
    pair = lax.axis_index("pair")
    level = lax.axis_index("plane")
    offset = (lax.axis_index("space") * 2 + pair) * own
    e_x, e_y, e_z = (
        jnp.asarray(eigen_values(n).astype(np.float32)) for n in (width_x, width_y, width_z)
    )
    spectrum = (
        e_x[None, :, None]
        + lax.dynamic_slice_in_dim(e_y, offset, own)[:, None, None]
        + e_z[None, None, :]
    )
    fine = (1.0 + half * spectrum) / (1.0 - half * spectrum)
    wide = steps * half
    coarse = (1.0 + wide * spectrum) / (1.0 - wide * spectrum)
    leap = fine
    for _ in range(steps - 1):
        leap = leap * fine

    def swap(fields):
        return lax.all_to_all(fields, ("space", "pair"), split_axis=0, concat_axis=0, tiled=True)

    def spread(fields):
        return swap(fields).reshape(n_space, 2, *fields.shape[1:])

    by_device = table_x.reshape(n_space, planes, width_x)

    def modes(cells):
        return jnp.einsum("sbmqr,smp->bqpr", cells, by_device, precision=high)

    share = planes // 2
    opened = opening_fields(coarse_guess[0], initial, z_right, y_left, pair, parts)
    opened, forcing = lax.optimization_barrier((opened, forcing))
    opened = spread(opened)
    pushed, relaxed = front(
        forcing, z_right, y_scaled, jnp.asarray(fine_pivots.reshape(-1, parts, own, width_z)), parts
    )
    opened, relaxed = lax.optimization_barrier((opened, relaxed))
    arrived = spread(relaxed)

    guess = modes(opened[:, :, :planes])
    before = lax.ppermute(guess[1], "plane", [(i, (i + 1) % n_plane) for i in range(n_plane)])
    anchor = jnp.einsum(
        "sbmqr,sbmp->qpr",
        opened[:, :, planes:],
        table_x.reshape(n_space, 2, share, width_x),
        precision=high,
    )

    full = np.concatenate([np.zeros((1, width_x)), sine_table(width_x), np.zeros((1, width_x))])
    across = np.stack([full[0:width_x:planes], full[planes + 1 :: planes]], axis=1)
    across = across.astype(np.float32)
    x_left = jnp.asarray(left_table(sine_table(width_x)))
    ghost_left = jnp.asarray(ghost_table(across, steps))
    kick_left = jnp.asarray(kick_table(across, steps))
    value, second_residual, beyond = modal(
        arrived, before, guess, spectrum, (x_left, kick_left, ghost_left)
    )

    def chunk_of(array, c):
        return lax.slice_in_dim(array, c * rows, (c + 1) * rows, axis=0)

    shifted = [
        lax.ppermute(chunk_of(value[1], c), "plane", [(i, i + 1) for i in range(n_plane - 1)])
        for c in range(chunks)
    ]
    rate = [chunk_of(coarse, c) for c in range(chunks)]
    second = [chunk_of(second_residual, c) for c in range(chunks)]
    start = [chunk_of(before, c) for c in range(chunks)]
    carries = [jnp.zeros_like(start[0])] * chunks
    lasts, firsts, sent = [], [], []

    def onward(c, carried):
        return rate[c] * (rate[c] * carried + firsts[c]) + second[c]

    def hop(c, sent, place):
        return lax.ppermute(sent, "plane", [(place, place + 1)])

    swapped = []
    for c in range(chunks):
        if c > 0:
            sent[c - 1], start[c] = lax.optimization_barrier((sent[c - 1], start[c]))
        lasts.append(jnp.where(level == 0, chunk_of(anchor, c), shifted[c]))
        firsts.append(chunk_of(leap, c) * (lasts[c] - start[c]))
        sent.append(onward(c, carries[c]))
        other = jnp.where(pair == 0, second[c], firsts[c])
        swapped.append(lax.ppermute(other, "pair", [(0, 1), (1, 0)]))
    carries[0] = carries[0] + hop(0, sent[0], 0)
    following = onward(0, carries[0])
    following, lasts, swapped = lax.optimization_barrier((following, lasts, swapped))
    tables = (x_left, ghost_left)
    early = swap(to_cells(None, spectrum, tables, n_space, steps, lasts, (value, beyond)))
    for place in range(n_plane - 1):
        for c in range(chunks):
            if place > 0:
                sent[c] = following if place + c == 1 else onward(c, carries[c])
            if c < chunks - 1:
                sent[c], second[c + 1] = lax.optimization_barrier((sent[c], second[c + 1]))
            if c == chunks - 1 and place == n_plane - 2:
                sent[c], pushed = lax.optimization_barrier((sent[c], pushed))
            if place + c > 0:
                carries[c] = carries[c] + hop(c, sent[c], place)
    mine = jnp.where(pair == 0, jnp.concatenate(firsts, axis=0), second_residual)
    other = jnp.concatenate(swapped, axis=0)
    fine_pivots, wide_pivots = (
        jnp.asarray(a.reshape(-1, parts, own, width_z)) for a in (fine_pivots, wide_pivots)
    )
    early, firsts = lax.optimization_barrier((early, firsts))
    lates = []
    for c in range(chunks):
        late = to_cells(
            wide, chunk_of(spectrum, c), tables, n_space, steps, carries[c : c + 1], (firsts[c],)
        )
        late, mine = lax.optimization_barrier((late, mine))
        lates.append(swap(late))
    residual = jnp.concatenate(
        [jnp.where(pair == 0, mine, other), jnp.where(pair == 0, other, mine)], axis=0
    ).transpose(1, 0, 2)
    pushed = pushed.reshape(steps, planes, parts, own, width_z)
    points = finish(pushed, early, lates, fine_pivots, wide_pivots, y_left, z_right)
    return (points, residual[None])


def solution(mesh):
    whole = mesh.devices
    cut = Mesh(whole.reshape(whole.shape[0] // 2, 2, whole.shape[1]), ("plane", "pair", "space"))
    both = ("plane", "pair")
    placed = (P(both, "space", None, None), P(both, "space", None, None), P("space", None, None))
    return jax.shard_map(
        per_device,
        mesh=cut,
        in_specs=placed,
        out_specs=(P(both, "space", None, None), P(both, None, "space", None)),
        check_vma=False,
    )
```
